256 devices in a mesh: ep: 8 (over y, core), tm: 32 (over z, x).
Axes of the slice: x: 4, y: 4, z: 8, core: 2. Of those that a mesh axis runs over, the one named last changes fastest.
Arguments:
- observed: float32 [2048, 4096, 32], P('ep', 'tm'), may hold values from -27 to 27
- missing: int32 [2048, 4096, 32], P('ep', 'tm'), may hold values 0 or 1
- episode_init: float32 [2048, 256], P(('ep', 'tm')), may hold values from -2 to 2
- time_init: float32 [4096, 256], P(('tm', 'ep')), may hold values from -2 to 2
- channel: float32 [32, 256], replicated, may hold values from -0.5 to 1.5
Outputs:
- imputed: float32 [2048, 4096, 32], P('ep', 'tm')
The draws below stay inside these ranges and needn't reach their ends.
All inputs are finite; a program needn't handle non-finite values. No bound on the sum of `missing` on one device may be relied on, other than what follows from the above.
Results may differ from the reference program's by a relative error of at most 0.0003.
Values sent between devices are 32-bit elements; how exact they have to be, the bound alone decides.
A program may use at most 128 MiB of HBM per device.

```python
import jax
import jax.numpy as jnp
from jax import lax

K = 32
R = 256
SWEEPS = 2
EPISODES = 2048
TIMES = 4096


def draw_observed(key, part):
    key = jax.random.fold_in(key, 7)
    keys = jax.random.split(key, 4)
    ep_parts = jax.random.uniform(keys[0], (4, EPISODES), minval=-1.5, maxval=1.5)
    tm_parts = jax.random.uniform(keys[1], (4, TIMES), minval=-1.5, maxval=1.5)
    ch_parts = jax.random.uniform(keys[2], (4, K), minval=-1.5, maxval=1.5)
    signal = jnp.zeros((EPISODES, TIMES, K), jnp.float32)
    for term in range(4):
        signal = signal + ep_parts[term][:, None, None] * tm_parts[term][None, :, None] * ch_parts[term][None, None, :]
    noise = jax.random.uniform(keys[3], (EPISODES, TIMES, K), minval=-1.0, maxval=1.0)
    total = 0.5 * signal + noise
    return total.astype(jnp.float32)


def draw_time_init(key, part):
    key = jax.random.fold_in(key, 11)
    keys = jax.random.split(key, 4)
    signs = jnp.where(jax.random.bernoulli(keys[0], 0.5, (TIMES,)), 1.0, -1.0)
    weights = signs * jax.random.uniform(keys[1], (TIMES,), minval=0.6, maxval=1.4)
    common = jnp.clip(jax.random.normal(keys[2], (R,)), -2.5, 2.5)
    noise = 0.1 * jax.random.normal(keys[3], (TIMES, R))
    total = 0.5 * weights[:, None] * common[None, :] + noise
    return jnp.clip(total, -2.0, 2.0).astype(jnp.float32)


def set_ends(array, key, smallest, high):
    index_at = [jax.random.randint(jax.random.fold_in(key, axis), (), 0, length) for axis, length in enumerate(array.shape)]
    main_axis = array.shape.index(max(array.shape))
    beside = index_at[:main_axis] + [(index_at[main_axis] + 1) % array.shape[main_axis]] + index_at[main_axis + 1:]
    return array.at[tuple(index_at)].set(smallest).at[tuple(beside)].set(high)


def block_scale(own_key, extent, pieces, least, top_value):
    def one(dim, blocks):
        draws = jax.random.uniform(jax.random.fold_in(jax.random.fold_in(own_key, 6), dim), (blocks,), jnp.float32, least / len(pieces), top_value / len(pieces))
        return jnp.repeat(jnp.exp(draws), extent[dim] // blocks).reshape((-1,) + (1,) * (len(extent) - dim - 1))

    level = one(*pieces[0])
    for cut in pieces[1:]:
        level = level * one(*cut)
    return level


def normal_values(stream_key, shape, deviation, most, shards=(), kind=jnp.bfloat16):
    values = deviation * jax.random.normal(stream_key, shape, jnp.float32)
    if shards:
        values = values * block_scale(stream_key, shape, shards, -0.22, 0.18)
    return jnp.clip(values, -most, most).astype(kind)


def setup_inputs(seed: int = 0) -> dict:
    streams_of = jax.random.split(jax.random.key(seed), 6)
    return {
        "observed": draw_observed(jax.random.fold_in(streams_of[5], 71), 0),
        "missing": set_ends((jax.random.randint(streams_of[1], (EPISODES, TIMES, K), 0, 2) < 1).astype(jnp.int32), jax.random.fold_in(streams_of[1], 1), 0, 1),
        "episode_init": normal_values(streams_of[2], (EPISODES, R), 0.3, 2.0, ((0, 256),), jnp.float32),
        "time_init": draw_time_init(jax.random.fold_in(streams_of[5], 71), 0),
        "channel": jnp.clip(jax.random.uniform(streams_of[4], (K, R), jnp.float32, -0.5, 1.5), -0.5, 1.5),
    }


ridge_weight = 1.0
HIGH = lax.Precision.HIGHEST

def khatri(left, channel):
    return (left[:, None, :] * channel[None, :, :]).reshape(-1, left.shape[1])

def gram_rows(rows):
    return lax.dot_general(rows.astype(jnp.float32), rows.astype(jnp.float32), (((0,), (0,)), ((), ())), precision=HIGH, preferred_element_type=jnp.float32)

def solve_rows(gram_other, gram_c, moments):
    system = gram_other * gram_c + ridge_weight * jnp.eye(gram_c.shape[0], dtype=jnp.float32)
    lower = jnp.linalg.cholesky(system)
    return jax.scipy.linalg.cho_solve((lower, True), moments.T).T

def complete(flat_obs, flat_miss, a_full, basis):
    model = lax.dot_general(a_full.astype(jnp.float32), basis.astype(jnp.float32), (((1,), (1,)), ((), ())), precision=HIGH, preferred_element_type=jnp.float32)
    return jnp.where(flat_miss == 1, model, flat_obs)

def reference(observed, missing, episode_init, time_init, channel):
    flat_obs = observed.reshape(EPISODES, TIMES * K)
    flat_miss = missing.reshape(EPISODES, TIMES * K)
    gram_c = gram_rows(channel)
    a_full = episode_init
    b_full = time_init
    for sweep in range(SWEEPS):
        basis = khatri(b_full, channel)
        filled = complete(flat_obs, flat_miss, a_full, basis)
        moments_e = jnp.dot(filled.astype(jnp.float32), basis.astype(jnp.float32), precision=HIGH, preferred_element_type=jnp.float32)
        a_full = solve_rows(gram_rows(b_full), gram_c, moments_e)
        part = lax.dot_general(filled.astype(jnp.float32), a_full.astype(jnp.float32), (((0,), (0,)), ((), ())), precision=HIGH, preferred_element_type=jnp.float32)
        moments_t = jnp.sum(part.reshape(TIMES, K, R) * channel[None, :, :], axis=1)
        b_full = solve_rows(gram_rows(a_full), gram_c, moments_t)
    basis = khatri(b_full, channel)
    filled = complete(flat_obs, flat_miss, a_full, basis)
    return filled.reshape(EPISODES, TIMES, K)
```

```python
import functools

import jax
import jax.numpy as jnp
from jax import lax
from jax.experimental import pallas as pl
from jax.experimental.pallas import tpu as pltpu
from jax.sharding import PartitionSpec as P

SWEEPS = 2
RIDGE = 1.0
HIGH = lax.Precision.HIGHEST
F32 = jnp.float32
BF16 = jnp.bfloat16
MESH = pl.DeviceIdType.MESH

RANK = 256
WIDTH = 32
N_EP = 8
N_TM = 32
N_X = 4
I_BLK = 256
J_BLK = 128
ROWS = I_BLK * WIDTH
STEP_I = 8
CHUNK = STEP_I * WIDTH
N_CHUNK = ROWS // CHUNK
A_OWN = 8
B_OWN = 16
PIECE = 8
VMEM_LIMIT = 56 * 1024 * 1024


def dot(left, right):
    return lax.dot_general(
        left, right, (((1,), (0,)), ((), ())), preferred_element_type=F32
    )


def dot_high(left, right):
    return lax.dot_general(
        left, right, (((1,), (0,)), ((), ())), precision=HIGH, preferred_element_type=F32
    )


def split2(x):
    high = x.astype(BF16)
    return high, (x - high.astype(F32)).astype(BF16)


def split3(x):
    high = x.astype(BF16)
    rest = x - high.astype(F32)
    mid = rest.astype(BF16)
    return high, mid, (rest - mid.astype(F32)).astype(BF16)


def dot_packed(left, right):
    a0, a1, a2 = split3(left)
    b0, b1, b2 = split3(right)
    lhs = jnp.concatenate([a0, a0, a1, a0, a2, a1], axis=1)
    rhs = jnp.concatenate([b0, b1, b0, b2, b0, b1], axis=0)
    return dot(lhs, rhs)


def invert8(cols):
    row = lax.broadcasted_iota(jnp.int32, (8, 128), 0)
    for s in range(8):
        here = row == s
        at_s = [jnp.broadcast_to(cols[q][s : s + 1, :], (8, 128)) for q in range(8)]
        inv = 1.0 / at_s[s]
        pivot = cols[s]
        fresh = []
        for q in range(8):
            if q == s:
                fresh.append(jnp.where(here, inv, -pivot * inv))
            else:
                scaled = at_s[q] * inv
                fresh.append(jnp.where(here, scaled, cols[q] - pivot * scaled))
        cols = fresh
    return cols


def spread_row(x, m):
    return jnp.broadcast_to(x[m : m + 1, :], (8, 128))


def eliminate_panel(ref, r0, depth, n):
    tiles = n // 128
    groups = depth // 8
    lane = lax.broadcasted_iota(jnp.int32, (8, 128), 1)
    row = lax.broadcasted_iota(jnp.int32, (8, 128), 0)
    x = [
        [ref[r0 + 8 * v : r0 + 8 * v + 8, 128 * t : 128 * t + 128] for t in range(tiles)]
        for v in range(groups)
    ]
    for g in range(groups):
        t_piv, l0 = divmod(r0 + 8 * g, 128)

        def column(block, q):
            return jnp.broadcast_to(block[:, l0 + q : l0 + q + 1], (8, 128))

        inv = invert8([column(x[g][t_piv], q) for q in range(8)])
        inside = (lane >= l0) & (lane < l0 + 8)
        unit = jnp.where(lane - l0 == row, 1.0, 0.0)
        fresh = []
        for t in range(tiles):
            old = x[g][t]
            if t == t_piv:
                old = jnp.where(inside, unit, old)
            y = [inv[m] * spread_row(old, m) for m in range(8)]
            fresh.append(((y[0] + y[1]) + (y[2] + y[3])) + ((y[4] + y[5]) + (y[6] + y[7])))
        for v in range(groups):
            if v == g:
                continue
            cols = [column(x[v][t_piv], m) for m in range(8)]
            for t in range(tiles):
                old = x[v][t]
                if t == t_piv:
                    old = jnp.where(inside, 0.0, old)
                y = [cols[m] * spread_row(fresh[t], m) for m in range(8)]
                x[v][t] = old - (
                    ((y[0] + y[1]) + (y[2] + y[3])) + ((y[4] + y[5]) + (y[6] + y[7]))
                )
        x[g] = fresh
    for v in range(groups):
        for t in range(tiles):
            ref[r0 + 8 * v : r0 + 8 * v + 8, 128 * t : 128 * t + 128] = x[v][t]


def invert_in_place(ref, n, depth):
    for k in range(n // depth):
        r0 = k * depth
        eliminate_panel(ref, r0, depth, n)
        panel = ref[r0 : r0 + depth, :]
        lane = lax.broadcasted_iota(jnp.int32, (1, n), 1)
        inside = (lane >= r0) & (lane < r0 + depth)
        for lo, hi in ((0, r0), (r0 + depth, n)):
            if hi > lo:
                cols = ref[lo:hi, r0 : r0 + depth]
                ref[lo:hi, :] = jnp.where(inside, 0.0, ref[lo:hi, :]) - dot_packed(cols, panel)


def solve_kernel(g_ref, gc_ref, m_ref, out_ref, s_ref):
    n = RANK
    eye = lax.broadcasted_iota(jnp.int32, (n, n), 0) == lax.broadcasted_iota(jnp.int32, (n, n), 1)
    s_ref[...] = g_ref[...] * gc_ref[...] + jnp.where(eye, RIDGE, 0.0)
    invert_in_place(s_ref, n, 32)
    out_ref[...] = dot_high(m_ref[...], s_ref[...])


def solve_rows(gram, gram_c, moments):
    return pl.pallas_call(
        solve_kernel,
        out_shape=jax.ShapeDtypeStruct(moments.shape, F32),
        in_specs=[pl.BlockSpec(memory_space=pltpu.VMEM)] * 3,
        out_specs=pl.BlockSpec(memory_space=pltpu.VMEM),
        scratch_shapes=[pltpu.VMEM((RANK, RANK), F32)],
        name="solve",
    )(gram, gram_c, moments)


def coords():
    e = lax.axis_index("ep")
    t = lax.axis_index("tm")
    return e, t, t // N_X, t % N_X


def greet(tm_group, ep_group, layer_group):
    e, t, z, x = coords()
    barrier = pltpu.get_barrier_semaphore()
    count = 0
    if tm_group:

        def body(k, _):
            peer = lax.rem(t + k, N_TM)
            pl.semaphore_signal(barrier, inc=1, device_id=(e, peer), device_id_type=MESH)
            return 0

        lax.fori_loop(1, N_TM, body, 0)
        count += N_TM - 1
    if layer_group:

        def body(k, _):
            pe = lax.rem(e + k // N_X, N_EP)
            px = lax.rem(x + k % N_X, N_X)
            pl.semaphore_signal(barrier, inc=1, device_id=(pe, z * N_X + px), device_id_type=MESH)
            return 0

        lax.fori_loop(1, N_EP * N_X, body, 0)
        count += N_EP * N_X - 1
    elif ep_group:

        def body(k, _):
            peer = lax.rem(e + k, N_EP)
            pl.semaphore_signal(barrier, inc=1, device_id=(peer, t), device_id_type=MESH)
            return 0

        lax.fori_loop(1, N_EP, body, 0)
        count += N_EP - 1
    pl.semaphore_wait(barrier, count)


def send_tm(src_of, dst, send_sem, recv_sem):
    e, t, _, _ = coords()

    def body(k, _):
        peer = lax.rem(t + k, N_TM)
        pltpu.make_async_remote_copy(
            src_ref=src_of(peer),
            dst_ref=dst,
            send_sem=send_sem,
            recv_sem=recv_sem,
            device_id=(e, peer),
            device_id_type=MESH,
        ).start()
        return 0

    lax.fori_loop(1, N_TM, body, 0)


def send_ep(src_of, dst, send_sem, recv_sem):
    e, t, _, _ = coords()

    def body(k, _):
        peer = lax.rem(e + k, N_EP)
        pltpu.make_async_remote_copy(
            src_ref=src_of(peer),
            dst_ref=dst,
            send_sem=send_sem,
            recv_sem=recv_sem,
            device_id=(peer, t),
            device_id_type=MESH,
        ).start()
        return 0

    lax.fori_loop(1, N_EP, body, 0)


def send_layer(src, dst, send_sem, recv_sem):
    e, _, z, x = coords()

    def body(k, _):
        pe = lax.rem(e + k // N_X, N_EP)
        px = lax.rem(x + k % N_X, N_X)
        pltpu.make_async_remote_copy(
            src_ref=src,
            dst_ref=dst,
            send_sem=send_sem,
            recv_sem=recv_sem,
            device_id=(pe, z * N_X + px),
            device_id_type=MESH,
        ).start()
        return 0

    lax.fori_loop(1, N_EP * N_X, body, 0)


def settle(ref, sem):
    pltpu.make_async_copy(ref, ref, sem).wait()


def sum_slots(ref, slots, rows):
    parts = [ref[rows * s : rows * (s + 1), :] for s in range(slots)]
    while len(parts) > 1:
        parts = [parts[i] + parts[i + 1] for i in range(0, len(parts), 2)]
    return parts[0]


def scaled_rows(a_rows, chan):
    return jnp.concatenate([a_rows[i : i + 1, :] * chan for i in range(STEP_I)], axis=0)


def rows_at(index, size):
    return pl.ds(pl.multiple_of(index * size, size), size)


def model_chunk(a_rows, chan, wide, narrow):
    high, low = split2(scaled_rows(a_rows, chan))
    both = dot(high, wide)
    return (both[:, :J_BLK] + both[:, J_BLK:]) + dot(low, narrow)


def episode_kernel(
    first,
    obs_ref,
    miss_ref,
    a_ref,
    b_ref,
    chan_ref,
    filled_ref,
    m_ref,
    g_ref,
    x_buf,
    miss_buf,
    a_buf,
    b_buf,
    bt_buf,
    wide_buf,
    twice_buf,
    low_buf,
    gpart,
    grecv,
    gfull,
    part,
    mrecv,
    load_sem,
    send_sem,
    recv_sem,
):
    e, t, z, x = coords()
    load_x = pltpu.make_async_copy(obs_ref, x_buf, load_sem.at[0])
    load_m = pltpu.make_async_copy(miss_ref, miss_buf, load_sem.at[1])
    load_x.start()
    load_m.start()
    b_mine = rows_at(e, B_OWN)
    b_buf[b_mine, :] = b_ref[...]
    if first:
        a_mine = rows_at(t, A_OWN)
        a_buf[a_mine, :] = a_ref[...]
    greet(True, True, True)
    send_ep(lambda peer: b_buf.at[b_mine], b_buf.at[b_mine], send_sem.at[0], recv_sem.at[0])
    if first:
        send_tm(lambda peer: a_buf.at[a_mine], a_buf.at[a_mine], send_sem.at[1], recv_sem.at[1])
    others_b = b_buf.at[pl.ds(0, (N_EP - 1) * B_OWN)]
    settle(others_b, recv_sem.at[0])

    b = b_buf[...]
    bt = b.T
    bt_buf[...] = bt
    bt_high, bt_low = split2(bt)
    wide_buf[...] = jnp.concatenate([bt_high, bt_low], axis=1)
    b_high, b_low = split2(b)
    twice_buf[...] = jnp.concatenate([b_high, b_high], axis=0)
    low_buf[...] = b_low
    slab = N_X * PIECE
    gpart[...] = dot_high(bt_buf[rows_at(e, slab), :], b)
    g_slot = grecv.at[rows_at(t, PIECE)]
    send_tm(lambda peer: gpart.at[rows_at(peer % N_X, PIECE)], g_slot, send_sem.at[2], recv_sem.at[2])
    grecv[rows_at(t, PIECE), :] = gpart[rows_at(x, PIECE), :]
    if first:
        settle(a_buf.at[pl.ds(0, (N_TM - 1) * A_OWN)], recv_sem.at[1])
    load_x.wait()
    load_m.wait()

    def chunk(c, _):
        rows = rows_at(c, CHUNK)
        own = rows_at(c, STEP_I)
        chan = chan_ref[...]
        a_rows = a_buf[own, :] if first else a_ref[own, :]
        model = model_chunk(a_rows, chan, wide_buf[...], wide_buf[:, :J_BLK])
        filled = jnp.where(miss_buf[rows, :] == 1, model, x_buf[rows, :])
        x_buf[rows, :] = filled
        high, low = split2(filled)
        prod = dot(jnp.concatenate([high, low], axis=1), twice_buf[...]) + dot(high, low_buf[...])
        part[own, :] = jnp.sum(prod.reshape(STEP_I, WIDTH, RANK) * chan[None], axis=1)
        return 0

    lax.fori_loop(0, N_CHUNK // 2, chunk, 0)
    settle(grecv.at[pl.ds(0, (N_TM - 1) * PIECE)], recv_sem.at[2])
    g_mine = rows_at(e * N_X + x, PIECE)
    gfull[g_mine, :] = sum_slots(grecv, N_TM, PIECE)
    send_layer(gfull.at[g_mine], gfull.at[g_mine], send_sem.at[3], recv_sem.at[3])
    lax.fori_loop(N_CHUNK // 2, N_CHUNK, chunk, 0)
    save = pltpu.make_async_copy(x_buf, filled_ref, load_sem.at[2])
    save.start()
    m_slot = mrecv.at[rows_at(t, A_OWN)]
    send_tm(lambda peer: part.at[rows_at(peer, A_OWN)], m_slot, send_sem.at[4], recv_sem.at[4])
    mrecv[rows_at(t, A_OWN), :] = part[rows_at(t, A_OWN), :]
    settle(gfull.at[pl.ds(0, (N_EP * N_X - 1) * PIECE)], recv_sem.at[3])
    g_ref[...] = gfull[...]
    settle(mrecv.at[pl.ds(0, (N_TM - 1) * A_OWN)], recv_sem.at[4])
    m_ref[...] = sum_slots(mrecv, N_TM, A_OWN)
    save.wait()
    settle(others_b, send_sem.at[0])
    if first:
        settle(a_buf.at[pl.ds(0, (N_TM - 1) * A_OWN)], send_sem.at[1])
    settle(grecv.at[pl.ds(0, (N_TM - 1) * PIECE)], send_sem.at[2])
    settle(gfull.at[pl.ds(0, (N_EP * N_X - 1) * PIECE)], send_sem.at[3])
    settle(mrecv.at[pl.ds(0, (N_TM - 1) * A_OWN)], send_sem.at[4])


def episode_step(first, obs, miss, a, b_own, channel):
    vmem = pl.BlockSpec(memory_space=pltpu.VMEM)
    anywhere = pl.BlockSpec(memory_space=pl.ANY)
    return pl.pallas_call(
        functools.partial(episode_kernel, first),
        out_shape=(
            jax.ShapeDtypeStruct((ROWS, J_BLK), F32),
            jax.ShapeDtypeStruct((A_OWN, RANK), F32),
            jax.ShapeDtypeStruct((RANK, RANK), F32),
        ),
        in_specs=[anywhere, anywhere, vmem, vmem, vmem],
        out_specs=(anywhere, vmem, vmem),
        scratch_shapes=[
            pltpu.VMEM((ROWS, J_BLK), F32),
            pltpu.VMEM((ROWS, J_BLK), jnp.int32),
            pltpu.VMEM((I_BLK, RANK), F32),
            pltpu.VMEM((J_BLK, RANK), F32),
            pltpu.VMEM((RANK, J_BLK), F32),
            pltpu.VMEM((RANK, 2 * J_BLK), BF16),
            pltpu.VMEM((2 * J_BLK, RANK), BF16),
            pltpu.VMEM((J_BLK, RANK), BF16),
            pltpu.VMEM((N_X * PIECE, RANK), F32),
            pltpu.VMEM((N_TM * PIECE, RANK), F32),
            pltpu.VMEM((RANK, RANK), F32),
            pltpu.VMEM((I_BLK, RANK), F32),
            pltpu.VMEM((I_BLK, RANK), F32),
            pltpu.SemaphoreType.DMA((3,)),
            pltpu.SemaphoreType.DMA((5,)),
            pltpu.SemaphoreType.DMA((5,)),
        ],
        compiler_params=pltpu.CompilerParams(
            collective_id=0 if first else 1,
            has_side_effects=True,
            vmem_limit_bytes=VMEM_LIMIT,
        ),
        name="episode_first" if first else "episode",
    )(obs, miss, a, b_own, channel)


def time_kernel(
    filled_ref,
    a_ref,
    chan_ref,
    ablk_ref,
    m_ref,
    g_ref,
    x_buf,
    a_buf,
    at_buf,
    gpart,
    grecv,
    gfull,
    part,
    mrecv,
    load_sem,
    send_sem,
    recv_sem,
):
    e, t, z, x = coords()
    load_x = pltpu.make_async_copy(filled_ref, x_buf, load_sem.at[0])
    load_x.start()
    a_mine = rows_at(t, A_OWN)
    a_buf[a_mine, :] = a_ref[...]
    greet(True, True, True)
    send_tm(lambda peer: a_buf.at[a_mine], a_buf.at[a_mine], send_sem.at[0], recv_sem.at[0])
    others_a = a_buf.at[pl.ds(0, (N_TM - 1) * A_OWN)]
    settle(others_a, recv_sem.at[0])

    a = a_buf[...]
    ablk_ref[...] = a
    at_buf[...] = a.T
    gpart[...] = dot_high(at_buf[rows_at(x, N_EP * PIECE), :], a)
    g_slot = grecv.at[rows_at(e, PIECE)]
    send_ep(lambda peer: gpart.at[rows_at(peer, PIECE)], g_slot, send_sem.at[1], recv_sem.at[1])
    grecv[rows_at(e, PIECE), :] = gpart[rows_at(e, PIECE), :]
    load_x.wait()
    part[...] = jnp.zeros_like(part)

    def chunk(c, _):
        high, low = split2(x_buf[rows_at(c, CHUNK), :])
        ac_high, ac_low = split2(scaled_rows(a_buf[rows_at(c, STEP_I), :], chan_ref[...]))
        high_t = high.T
        both = dot(jnp.concatenate([high_t, low.T], axis=0), ac_high)
        part[...] += (both[:J_BLK] + both[J_BLK:]) + dot(high_t, ac_low)
        return 0

    lax.fori_loop(0, N_CHUNK // 2, chunk, 0)
    settle(grecv.at[pl.ds(0, (N_EP - 1) * PIECE)], recv_sem.at[1])
    g_mine = rows_at(x * N_EP + e, PIECE)
    gfull[g_mine, :] = sum_slots(grecv, N_EP, PIECE)
    send_layer(gfull.at[g_mine], gfull.at[g_mine], send_sem.at[2], recv_sem.at[2])
    lax.fori_loop(N_CHUNK // 2, N_CHUNK, chunk, 0)
    m_slot = mrecv.at[rows_at(e, B_OWN)]
    send_ep(lambda peer: part.at[rows_at(peer, B_OWN)], m_slot, send_sem.at[3], recv_sem.at[3])
    mrecv[rows_at(e, B_OWN), :] = part[rows_at(e, B_OWN), :]
    settle(gfull.at[pl.ds(0, (N_EP * N_X - 1) * PIECE)], recv_sem.at[2])
    g_ref[...] = gfull[...]
    settle(mrecv.at[pl.ds(0, (N_EP - 1) * B_OWN)], recv_sem.at[3])
    m_ref[...] = sum_slots(mrecv, N_EP, B_OWN)
    settle(others_a, send_sem.at[0])
    settle(grecv.at[pl.ds(0, (N_EP - 1) * PIECE)], send_sem.at[1])
    settle(gfull.at[pl.ds(0, (N_EP * N_X - 1) * PIECE)], send_sem.at[2])
    settle(mrecv.at[pl.ds(0, (N_EP - 1) * B_OWN)], send_sem.at[3])


def time_step(filled, a_own, channel):
    vmem = pl.BlockSpec(memory_space=pltpu.VMEM)
    anywhere = pl.BlockSpec(memory_space=pl.ANY)
    return pl.pallas_call(
        time_kernel,
        out_shape=(
            jax.ShapeDtypeStruct((I_BLK, RANK), F32),
            jax.ShapeDtypeStruct((B_OWN, RANK), F32),
            jax.ShapeDtypeStruct((RANK, RANK), F32),
        ),
        in_specs=[anywhere, vmem, vmem],
        out_specs=(vmem, vmem, vmem),
        scratch_shapes=[
            pltpu.VMEM((ROWS, J_BLK), F32),
            pltpu.VMEM((I_BLK, RANK), F32),
            pltpu.VMEM((RANK, I_BLK), F32),
            pltpu.VMEM((N_EP * PIECE, RANK), F32),
            pltpu.VMEM((N_EP * PIECE, RANK), F32),
            pltpu.VMEM((RANK, RANK), F32),
            pltpu.VMEM((J_BLK, RANK), F32),
            pltpu.VMEM((J_BLK, RANK), F32),
            pltpu.SemaphoreType.DMA((1,)),
            pltpu.SemaphoreType.DMA((4,)),
            pltpu.SemaphoreType.DMA((4,)),
        ],
        compiler_params=pltpu.CompilerParams(
            collective_id=2, has_side_effects=True, vmem_limit_bytes=VMEM_LIMIT
        ),
        name="time",
    )(filled, a_own, channel)


def gather_kernel(b_ref, out_ref, b_buf, send_sem, recv_sem):
    e = lax.axis_index("ep")
    b_mine = rows_at(e, B_OWN)
    b_buf[b_mine, :] = b_ref[...]
    greet(False, True, False)
    send_ep(lambda peer: b_buf.at[b_mine], b_buf.at[b_mine], send_sem.at[0], recv_sem.at[0])
    others_b = b_buf.at[pl.ds(0, (N_EP - 1) * B_OWN)]
    settle(others_b, recv_sem.at[0])
    out_ref[...] = b_buf[...]
    settle(others_b, send_sem.at[0])


def gather_time(b_own):
    return pl.pallas_call(
        gather_kernel,
        out_shape=jax.ShapeDtypeStruct((J_BLK, RANK), F32),
        in_specs=[pl.BlockSpec(memory_space=pltpu.VMEM)],
        out_specs=pl.BlockSpec(memory_space=pltpu.VMEM),
        scratch_shapes=[
            pltpu.VMEM((J_BLK, RANK), F32),
            pltpu.SemaphoreType.DMA((1,)),
            pltpu.SemaphoreType.DMA((1,)),
        ],
        compiler_params=pltpu.CompilerParams(collective_id=3, has_side_effects=True),
        name="gather_time",
    )(b_own)


GRID = 8


def complete_kernel(obs_ref, miss_ref, a_ref, b_ref, chan_ref, out_ref, wide_buf):
    @pl.when(pl.program_id(0) == 0)
    def _():
        high, low = split2(b_ref[...].T)
        wide_buf[...] = jnp.concatenate([high, low], axis=1)

    chan = chan_ref[...]

    def chunk(c, _):
        rows = rows_at(c, CHUNK)
        model = model_chunk(a_ref[rows_at(c, STEP_I), :], chan, wide_buf[...], wide_buf[:, :J_BLK])
        out_ref[rows, :] = jnp.where(miss_ref[rows, :] == 1, model, obs_ref[rows, :])
        return 0

    lax.fori_loop(0, N_CHUNK // GRID, chunk, 0)


def complete(obs, miss, a_block, b_block, channel):
    rows = ROWS // GRID
    return pl.pallas_call(
        complete_kernel,
        grid=(GRID,),
        out_shape=jax.ShapeDtypeStruct((ROWS, J_BLK), F32),
        in_specs=[
            pl.BlockSpec((rows, J_BLK), lambda i: (i, 0)),
            pl.BlockSpec((rows, J_BLK), lambda i: (i, 0)),
            pl.BlockSpec((I_BLK // GRID, RANK), lambda i: (i, 0)),
            pl.BlockSpec((J_BLK, RANK), lambda i: (0, 0)),
            pl.BlockSpec((WIDTH, RANK), lambda i: (0, 0)),
        ],
        out_specs=pl.BlockSpec((rows, J_BLK), lambda i: (i, 0)),
        scratch_shapes=[pltpu.VMEM((RANK, 2 * J_BLK), BF16)],
        compiler_params=pltpu.CompilerParams(vmem_limit_bytes=VMEM_LIMIT),
        name="complete",
    )(obs, miss, a_block, b_block, channel)


def on_device(observed, missing, episode_init, time_init, channel):
    obs = observed.transpose(0, 2, 1).reshape(ROWS, J_BLK)
    miss = missing.transpose(0, 2, 1).reshape(ROWS, J_BLK)
    gram_c = lax.dot_general(
        channel, channel, (((0,), (0,)), ((), ())), precision=HIGH, preferred_element_type=F32
    )
    a = episode_init
    b_own = time_init
    for sweep in range(SWEEPS):
        filled, m_own, gram = episode_step(sweep == 0, obs, miss, a, b_own, channel)
        a_own = solve_rows(gram, gram_c, m_own)
        a, m_own, gram = time_step(filled, a_own, channel)
        b_own = solve_rows(gram, gram_c, m_own)
    b = gather_time(b_own)
    out = complete(obs, miss, a, b, channel)
    return out.reshape(I_BLK, WIDTH, J_BLK).transpose(0, 2, 1)


def solution(mesh):
    in_specs = (
        P("ep", "tm", None),
        P("ep", "tm", None),
        P(("ep", "tm"), None),
        P(("tm", "ep"), None),
        P(),
    )
    return jax.shard_map(
        on_device, mesh=mesh, in_specs=in_specs, out_specs=P("ep", "tm", None), check_vma=False
    )
```

```python
import jax
import jax.numpy as jnp
from jax import lax
from jax.experimental import pallas as pl
from jax.experimental.pallas import tpu as pltpu
from jax.sharding import PartitionSpec as P

SWEEPS = 2
RIDGE = 1.0
HIGH = lax.Precision.HIGHEST
F32 = jnp.float32
BF16 = jnp.bfloat16
MESH = pl.DeviceIdType.MESH

RANK = 256
WIDTH = 32
N_EP = 8
N_TM = 32
N_X = 4
I_BLK = 256
J_BLK = 128
ROWS = I_BLK * WIDTH
GROUP = 8
N_GROUP = WIDTH // GROUP
G_ROWS = GROUP * I_BLK
A_OWN = 8
B_OWN = 16
PIECE = 8
VMEM_LIMIT = 56 * 1024 * 1024


def dot(left, right):
    return lax.dot_general(
        left, right, (((1,), (0,)), ((), ())), preferred_element_type=F32
    )


def dot_high(left, right):
    return lax.dot_general(
        left, right, (((1,), (0,)), ((), ())), precision=HIGH, preferred_element_type=F32
    )


def split2(x):
    high = x.astype(BF16)
    return high, (x - high.astype(F32)).astype(BF16)


def split3(x):
    high = x.astype(BF16)
    rest = x - high.astype(F32)
    mid = rest.astype(BF16)
    return high, mid, (rest - mid.astype(F32)).astype(BF16)


def dot_packed(left, right):
    a0, a1, a2 = split3(left)
    b0, b1, b2 = split3(right)
    lhs = jnp.concatenate([a0, a0, a1, a0, a2, a1], axis=1)
    rhs = jnp.concatenate([b0, b1, b0, b2, b0, b1], axis=0)
    return dot(lhs, rhs)


def invert8(cols):
    row = lax.broadcasted_iota(jnp.int32, (8, 128), 0)
    for s in range(8):
        here = row == s
        at_s = [jnp.broadcast_to(cols[q][s : s + 1, :], (8, 128)) for q in range(8)]
        inv = 1.0 / at_s[s]
        pivot = cols[s]
        fresh = []
        for q in range(8):
            if q == s:
                fresh.append(jnp.where(here, inv, -pivot * inv))
            else:
                scaled = at_s[q] * inv
                fresh.append(jnp.where(here, scaled, cols[q] - pivot * scaled))
        cols = fresh
    return cols


def spread_row(x, m):
    return jnp.broadcast_to(x[m : m + 1, :], (8, 128))


def eliminate_panel(ref, r0, depth, n):
    tiles = n // 128
    groups = depth // 8
    lane = lax.broadcasted_iota(jnp.int32, (8, 128), 1)
    row = lax.broadcasted_iota(jnp.int32, (8, 128), 0)
    x = [
        [ref[r0 + 8 * v : r0 + 8 * v + 8, 128 * t : 128 * t + 128] for t in range(tiles)]
        for v in range(groups)
    ]
    for g in range(groups):
        t_piv, l0 = divmod(r0 + 8 * g, 128)

        def column(block, q):
            return jnp.broadcast_to(block[:, l0 + q : l0 + q + 1], (8, 128))

        inv = invert8([column(x[g][t_piv], q) for q in range(8)])
        inside = (lane >= l0) & (lane < l0 + 8)
        unit = jnp.where(lane - l0 == row, 1.0, 0.0)
        fresh = []
        for t in range(tiles):
            old = x[g][t]
            if t == t_piv:
                old = jnp.where(inside, unit, old)
            y = [inv[m] * spread_row(old, m) for m in range(8)]
            fresh.append(((y[0] + y[1]) + (y[2] + y[3])) + ((y[4] + y[5]) + (y[6] + y[7])))
        for v in range(groups):
            if v == g:
                continue
            cols = [column(x[v][t_piv], m) for m in range(8)]
            for t in range(tiles):
                old = x[v][t]
                if t == t_piv:
                    old = jnp.where(inside, 0.0, old)
                y = [cols[m] * spread_row(fresh[t], m) for m in range(8)]
                x[v][t] = old - (
                    ((y[0] + y[1]) + (y[2] + y[3])) + ((y[4] + y[5]) + (y[6] + y[7]))
                )
        x[g] = fresh
    for v in range(groups):
        for t in range(tiles):
            ref[r0 + 8 * v : r0 + 8 * v + 8, 128 * t : 128 * t + 128] = x[v][t]


def invert_in_place(ref, n, depth):
    for k in range(n // depth):
        r0 = k * depth
        eliminate_panel(ref, r0, depth, n)
        panel = ref[r0 : r0 + depth, :]
        lane = lax.broadcasted_iota(jnp.int32, (1, n), 1)
        inside = (lane >= r0) & (lane < r0 + depth)
        for lo, hi in ((0, r0), (r0 + depth, n)):
            if hi > lo:
                cols = ref[lo:hi, r0 : r0 + depth]
                ref[lo:hi, :] = jnp.where(inside, 0.0, ref[lo:hi, :]) - dot_packed(cols, panel)


def coords():
    e = lax.axis_index("ep")
    t = lax.axis_index("tm")
    return e, t, t // N_X, t % N_X


def greet():
    e, t, z, x = coords()
    barrier = pltpu.get_barrier_semaphore()

    def along_tm(k, _):
        peer = lax.rem(t + k, N_TM)
        pl.semaphore_signal(barrier, inc=1, device_id=(e, peer), device_id_type=MESH)
        return 0

    def in_layer(k, _):
        pe = lax.rem(e + k // N_X, N_EP)
        px = lax.rem(x + k % N_X, N_X)
        pl.semaphore_signal(barrier, inc=1, device_id=(pe, z * N_X + px), device_id_type=MESH)
        return 0

    lax.fori_loop(1, N_TM, along_tm, 0)
    lax.fori_loop(N_X, N_EP * N_X, in_layer, 0)
    pl.semaphore_wait(barrier, N_TM - 1 + (N_EP - 1) * N_X)


def send_tm(src_of, dst, send_sem, recv_sem):
    e, t, _, _ = coords()

    def body(k, _):
        peer = lax.rem(t + k, N_TM)
        pltpu.make_async_remote_copy(
            src_ref=src_of(peer),
            dst_ref=dst,
            send_sem=send_sem,
            recv_sem=recv_sem,
            device_id=(e, peer),
            device_id_type=MESH,
        ).start()
        return 0

    lax.fori_loop(1, N_TM, body, 0)


def send_ep(src_of, dst, send_sem, recv_sem):
    e, t, _, _ = coords()

    def body(k, _):
        peer = lax.rem(e + k, N_EP)
        pltpu.make_async_remote_copy(
            src_ref=src_of(peer),
            dst_ref=dst,
            send_sem=send_sem,
            recv_sem=recv_sem,
            device_id=(peer, t),
            device_id_type=MESH,
        ).start()
        return 0

    lax.fori_loop(1, N_EP, body, 0)


def send_layer(src, dst, send_sem, recv_sem):
    e, _, z, x = coords()

    def body(k, _):
        pe = lax.rem(e + k // N_X, N_EP)
        px = lax.rem(x + k % N_X, N_X)
        pltpu.make_async_remote_copy(
            src_ref=src,
            dst_ref=dst,
            send_sem=send_sem,
            recv_sem=recv_sem,
            device_id=(pe, z * N_X + px),
            device_id_type=MESH,
        ).start()
        return 0

    lax.fori_loop(1, N_EP * N_X, body, 0)


def settle(ref, sem):
    pltpu.make_async_copy(ref, ref, sem).wait()


def sum_slots(ref, slots, rows):
    parts = [ref[rows * s : rows * (s + 1), :] for s in range(slots)]
    while len(parts) > 1:
        parts = [parts[i] + parts[i + 1] for i in range(0, len(parts), 2)]
    return parts[0]


def rows_at(index, size):
    return pl.ds(pl.multiple_of(index * size, size), size)


def dot_t(left, right):
    return lax.dot_general(
        left, right, (((1,), (1,)), ((), ())), preferred_element_type=F32
    )


def basis_pair(b, chan_ref, k):
    return split2(jnp.concatenate([b * chan_ref[pl.ds(k + d, 1), :] for d in range(2)], axis=0))


def model_pair(acat, high, low):
    return dot_t(acat, jnp.concatenate([high, high, low], axis=1))


def pack_left(x):
    high, low = split2(x)
    return jnp.concatenate([high, low, high], axis=1)


def fit_kernel(
    obs_ref,
    miss_ref,
    a_ref,
    b_ref,
    chan_ref,
    w_ref,
    aout_ref,
    bout_ref,
    w_buf,
    miss_buf,
    xh_buf,
    xl_buf,
    a_buf,
    b_buf,
    acat,
    spread,
    gram_c,
    s_buf,
    bt_buf,
    gb_part,
    gb_recv,
    gb_full,
    me_part,
    me_recv,
    at_buf,
    ga_part,
    ga_recv,
    ga_full,
    mt_part,
    mt_acc,
    mt_recv,
    load_sem,
    save_sem,
    send_sem,
    recv_sem,
):
    e, t, z, x = coords()
    for g in range(N_GROUP):
        for q in range(GROUP):
            k = g * GROUP + q
            to = pl.ds(k * I_BLK, I_BLK)
            pltpu.make_async_copy(obs_ref.at[:, k, :], w_buf.at[to], load_sem.at[g]).start()
            pltpu.make_async_copy(miss_ref.at[:, k, :], miss_buf.at[to], load_sem.at[N_GROUP + g]).start()
    a_mine = rows_at(t, A_OWN)
    b_mine = rows_at(e, B_OWN)
    a_buf[a_mine, :] = a_ref[...]
    b_buf[b_mine, :] = b_ref[...]
    others_a = a_buf.at[pl.ds(0, (N_TM - 1) * A_OWN)]
    others_b = b_buf.at[pl.ds(0, (N_EP - 1) * B_OWN)]
    others_gb = gb_recv.at[pl.ds(0, (N_TM - 1) * PIECE)]
    others_gb_full = gb_full.at[pl.ds(0, (N_EP * N_X - 1) * PIECE)]
    others_me = me_recv.at[pl.ds(0, (N_TM - 1) * A_OWN)]
    others_ga = ga_recv.at[pl.ds(0, (N_EP - 1) * PIECE)]
    others_ga_full = ga_full.at[pl.ds(0, (N_EP * N_X - 1) * PIECE)]
    others_mt = mt_recv.at[pl.ds(0, (N_EP - 1) * B_OWN)]

    def send_b():
        send_ep(lambda peer: b_buf.at[b_mine], b_buf.at[b_mine], send_sem.at[0], recv_sem.at[0])

    def send_a():
        send_tm(lambda peer: a_buf.at[a_mine], a_buf.at[a_mine], send_sem.at[1], recv_sem.at[1])

    greet()
    send_b()
    send_a()

    chan_t = chan_ref[...].T
    gram_c[...] = dot_high(chan_t, chan_ref[...])
    for g in range(N_GROUP):
        spread[g] = chan_t[:, g * GROUP : (g + 1) * GROUP]

    def mask_group(g, _):
        rows = rows_at(g, G_ROWS)
        settle(w_buf.at[rows], load_sem.at[g])
        settle(miss_buf.at[rows], load_sem.at[N_GROUP + g])

        def mask_part(q, _):
            part = rows_at(g * GROUP + q, I_BLK)
            w_buf[part, :] = jnp.where(miss_buf[part, :] == 1, jnp.nan, w_buf[part, :])
            return 0

        lax.fori_loop(0, GROUP, mask_part, 0)
        return 0

    lax.fori_loop(0, N_GROUP, mask_group, 0)
    save = pltpu.make_async_copy(w_buf, w_ref, save_sem.at[0])
    save.start()
    settle(others_a, recv_sem.at[1])
    settle(others_a, send_sem.at[1])

    def sweep(s, _):
        acat[...] = pack_left(a_buf[...])
        me_part[...] = jnp.zeros_like(me_part)
        settle(others_b, recv_sem.at[0])
        settle(others_b, send_sem.at[0])
        b = b_buf[...]
        bt_buf[...] = b.T
        gb_part[...] = dot_high(bt_buf[rows_at(e, N_X * PIECE), :], b)
        gb_slot = gb_recv.at[rows_at(t, PIECE)]
        send_tm(
            lambda peer: gb_part.at[rows_at(peer % N_X, PIECE)], gb_slot, send_sem.at[2], recv_sem.at[2]
        )
        gb_recv[rows_at(t, PIECE), :] = gb_part[rows_at(x, PIECE), :]

        def episode_group(g, _):
            for p in range(0, GROUP, 2):
                k = g * GROUP + p
                b_high, b_low = basis_pair(b_buf[...], chan_ref, k)
                model = model_pair(acat[...], b_high, b_low)
                highs, lows = [], []
                for d in range(2):
                    rows = rows_at(k + d, I_BLK)
                    w = w_buf[rows, :]
                    filled = jnp.where(w != w, model[:, d * J_BLK : (d + 1) * J_BLK], w)
                    high, low = split2(filled)
                    xh_buf[rows, :] = high
                    xl_buf[rows, :] = low
                    highs.append(high)
                    lows.append(low)
                high = jnp.concatenate(highs, axis=1)
                low = jnp.concatenate(lows, axis=1)
                me_part[...] += dot(
                    jnp.concatenate([high, low, high], axis=1),
                    jnp.concatenate([b_high, b_high, b_low], axis=0),
                )
            return 0

        lax.fori_loop(0, N_GROUP, episode_group, 0)
        me_slot = me_recv.at[rows_at(t, A_OWN)]
        send_tm(lambda peer: me_part.at[rows_at(peer, A_OWN)], me_slot, send_sem.at[4], recv_sem.at[4])
        me_recv[rows_at(t, A_OWN), :] = me_part[rows_at(t, A_OWN), :]
        settle(others_gb, recv_sem.at[2])
        gb_mine = rows_at(e * N_X + x, PIECE)
        gb_full[gb_mine, :] = sum_slots(gb_recv, N_TM, PIECE)
        send_layer(gb_full.at[gb_mine], gb_full.at[gb_mine], send_sem.at[3], recv_sem.at[3])
        settle(others_gb_full, recv_sem.at[3])
        form_system(s_buf, gb_full, gram_c)
        invert_in_place(s_buf, RANK, 32)
        settle(others_me, recv_sem.at[4])
        a_buf[a_mine, :] = dot_high(sum_slots(me_recv, N_TM, A_OWN), s_buf[...])
        send_a()
        settle(others_gb, send_sem.at[2])
        settle(others_gb_full, send_sem.at[3])
        settle(others_me, send_sem.at[4])

        settle(others_a, recv_sem.at[1])
        settle(others_a, send_sem.at[1])
        a = a_buf[...]
        at = a.T
        at_buf[...] = at
        ga_part[...] = dot_high(at_buf[rows_at(x, N_EP * PIECE), :], a)
        ga_slot = ga_recv.at[rows_at(e, PIECE)]
        send_ep(lambda peer: ga_part.at[rows_at(peer, PIECE)], ga_slot, send_sem.at[5], recv_sem.at[5])
        ga_recv[rows_at(e, PIECE), :] = ga_part[rows_at(e, PIECE), :]
        acat[...] = pack_left(at_buf[...])
        mt_acc[...] = jnp.zeros_like(mt_acc)

        def time_group(g, _):
            for p in range(0, GROUP, 2):
                k = g * GROUP + p
                high = jnp.concatenate([xh_buf[rows_at(k + d, I_BLK), :] for d in range(2)], axis=1)
                low = jnp.concatenate([xl_buf[rows_at(k + d, I_BLK), :] for d in range(2)], axis=1)
                prod = dot(acat[...], jnp.concatenate([high, high, low], axis=0))
                terms = [
                    jnp.broadcast_to(spread[g, :, p + d : p + d + 1], (RANK, J_BLK))
                    * prod[:, d * J_BLK : (d + 1) * J_BLK]
                    for d in range(2)
                ]
                mt_acc[...] += terms[0] + terms[1]
            return 0

        lax.fori_loop(0, N_GROUP, time_group, 0)
        mt_part[...] = mt_acc[...].T
        mt_slot = mt_recv.at[rows_at(e, B_OWN)]
        send_ep(lambda peer: mt_part.at[rows_at(peer, B_OWN)], mt_slot, send_sem.at[7], recv_sem.at[7])
        mt_recv[rows_at(e, B_OWN), :] = mt_part[rows_at(e, B_OWN), :]
        settle(others_ga, recv_sem.at[5])
        ga_mine = rows_at(x * N_EP + e, PIECE)
        ga_full[ga_mine, :] = sum_slots(ga_recv, N_EP, PIECE)
        send_layer(ga_full.at[ga_mine], ga_full.at[ga_mine], send_sem.at[6], recv_sem.at[6])
        settle(others_ga_full, recv_sem.at[6])
        form_system(s_buf, ga_full, gram_c)
        invert_in_place(s_buf, RANK, 32)
        settle(others_mt, recv_sem.at[7])
        b_buf[b_mine, :] = dot_high(sum_slots(mt_recv, N_EP, B_OWN), s_buf[...])
        send_b()
        settle(others_ga, send_sem.at[5])
        settle(others_ga_full, send_sem.at[6])
        settle(others_mt, send_sem.at[7])
        return 0

    lax.fori_loop(0, SWEEPS, sweep, 0)
    aout_ref[...] = a_buf[...]
    settle(others_b, recv_sem.at[0])
    settle(others_b, send_sem.at[0])
    bout_ref[...] = b_buf[...]
    save.wait()


def form_system(s_ref, gram_ref, gram_c):
    eye = lax.broadcasted_iota(jnp.int32, (RANK, RANK), 0) == lax.broadcasted_iota(
        jnp.int32, (RANK, RANK), 1
    )
    s_ref[...] = gram_ref[...] * gram_c[...] + jnp.where(eye, RIDGE, 0.0)


def fit(obs, miss, a_own, b_own, channel):
    vmem = pl.BlockSpec(memory_space=pltpu.VMEM)
    anywhere = pl.BlockSpec(memory_space=pl.ANY)

    def f32(*shape):
        return pltpu.VMEM(shape, F32)

    return pl.pallas_call(
        fit_kernel,
        out_shape=(
            jax.ShapeDtypeStruct((ROWS, J_BLK), F32),
            jax.ShapeDtypeStruct((I_BLK, RANK), F32),
            jax.ShapeDtypeStruct((J_BLK, RANK), F32),
        ),
        in_specs=[anywhere, anywhere, vmem, vmem, vmem],
        out_specs=(anywhere, vmem, vmem),
        scratch_shapes=[
            f32(ROWS, J_BLK),
            pltpu.VMEM((ROWS, J_BLK), jnp.int32),
            pltpu.VMEM((ROWS, J_BLK), BF16),
            pltpu.VMEM((ROWS, J_BLK), BF16),
            f32(I_BLK, RANK),
            f32(J_BLK, RANK),
            pltpu.VMEM((I_BLK, 3 * RANK), BF16),
            f32(N_GROUP, RANK, GROUP),
            f32(RANK, RANK),
            f32(RANK, RANK),
            f32(RANK, J_BLK),
            f32(N_X * PIECE, RANK),
            f32(N_TM * PIECE, RANK),
            f32(RANK, RANK),
            f32(I_BLK, RANK),
            f32(I_BLK, RANK),
            f32(RANK, I_BLK),
            f32(N_EP * PIECE, RANK),
            f32(N_EP * PIECE, RANK),
            f32(RANK, RANK),
            f32(J_BLK, RANK),
            f32(RANK, J_BLK),
            f32(J_BLK, RANK),
            pltpu.SemaphoreType.DMA((2 * N_GROUP,)),
            pltpu.SemaphoreType.DMA((1,)),
            pltpu.SemaphoreType.DMA((8,)),
            pltpu.SemaphoreType.DMA((8,)),
        ],
        compiler_params=pltpu.CompilerParams(
            collective_id=0, has_side_effects=True, vmem_limit_bytes=VMEM_LIMIT
        ),
        name="fit",
    )(obs, miss, a_own, b_own, channel)


def complete_kernel(w_ref, a_ref, b_ref, chan_ref, out_ref, w_buf, acat, load_sem, save_sem):
    for g in range(N_GROUP):
        rows = pl.ds(g * G_ROWS, G_ROWS)
        pltpu.make_async_copy(w_ref.at[rows], w_buf.at[rows], load_sem.at[g]).start()
    acat[...] = pack_left(a_ref[...])

    def group(g, _):
        settle(w_buf.at[rows_at(g, G_ROWS)], load_sem.at[g])
        for p in range(0, GROUP, 2):
            k = g * GROUP + p
            b_high, b_low = basis_pair(b_ref[...], chan_ref, k)
            model = model_pair(acat[...], b_high, b_low)
            for d in range(2):
                rows = rows_at(k + d, I_BLK)
                w = w_buf[rows, :]
                w_buf[rows, :] = jnp.where(w != w, model[:, d * J_BLK : (d + 1) * J_BLK], w)
        return 0

    for g in range(N_GROUP):
        group(g, 0)
        for q in range(GROUP):
            k = g * GROUP + q
            pltpu.make_async_copy(
                w_buf.at[pl.ds(k * I_BLK, I_BLK)], out_ref.at[:, k, :], save_sem.at[g]
            ).start()
    for g in range(N_GROUP):
        settle(w_buf.at[pl.ds(g * G_ROWS, G_ROWS)], save_sem.at[g])


def complete(w, a_block, b_block, channel):
    vmem = pl.BlockSpec(memory_space=pltpu.VMEM)
    anywhere = pl.BlockSpec(memory_space=pl.ANY)
    return pl.pallas_call(
        complete_kernel,
        out_shape=jax.ShapeDtypeStruct((I_BLK, WIDTH, J_BLK), F32),
        in_specs=[anywhere, vmem, vmem, vmem],
        out_specs=anywhere,
        scratch_shapes=[
            pltpu.VMEM((ROWS, J_BLK), F32),
            pltpu.VMEM((I_BLK, 3 * RANK), BF16),
            pltpu.SemaphoreType.DMA((N_GROUP,)),
            pltpu.SemaphoreType.DMA((N_GROUP,)),
        ],
        compiler_params=pltpu.CompilerParams(vmem_limit_bytes=VMEM_LIMIT),
        name="complete",
    )(w, a_block, b_block, channel)


def on_device(observed, missing, episode_init, time_init, channel):
    obs = observed.transpose(0, 2, 1)
    miss = missing.transpose(0, 2, 1)
    w, a, b = fit(obs, miss, episode_init, time_init, channel)
    return complete(w, a, b, channel).transpose(0, 2, 1)


def solution(mesh):
    in_specs = (
        P("ep", "tm", None),
        P("ep", "tm", None),
        P(("ep", "tm"), None),
        P(("tm", "ep"), None),
        P(),
    )
    return jax.shard_map(
        on_device, mesh=mesh, in_specs=in_specs, out_specs=P("ep", "tm", None), check_vma=False
    )
```

```python
import jax
import jax.numpy as jnp
from jax import lax
from jax.experimental import pallas as pl
from jax.experimental.pallas import tpu as pltpu
from jax.sharding import PartitionSpec as P

SWEEPS = 2
RIDGE = 1.0
HIGH = lax.Precision.HIGHEST
F32 = jnp.float32
BF16 = jnp.bfloat16
MESH = pl.DeviceIdType.MESH

RANK = 256
WIDTH = 32
N_EP = 8
N_TM = 32
N_X = 4
I_BLK = 256
J_BLK = 128
ROWS = I_BLK * WIDTH
GROUP = 8
N_GROUP = WIDTH // GROUP
G_ROWS = GROUP * I_BLK
A_OWN = 8
B_OWN = 16
PIECE = 8
VMEM_LIMIT = 56 * 1024 * 1024


def dot(left, right):
    return lax.dot_general(
        left, right, (((1,), (0,)), ((), ())), preferred_element_type=F32
    )


def dot_high(left, right):
    return lax.dot_general(
        left, right, (((1,), (0,)), ((), ())), precision=HIGH, preferred_element_type=F32
    )


def split2(x):
    high = x.astype(BF16)
    return high, (x - high.astype(F32)).astype(BF16)


def split3(x):
    high = x.astype(BF16)
    rest = x - high.astype(F32)
    mid = rest.astype(BF16)
    return high, mid, (rest - mid.astype(F32)).astype(BF16)


def dot_packed(left, right):
    a0, a1, a2 = split3(left)
    b0, b1, b2 = split3(right)
    lhs = jnp.concatenate([a0, a0, a1, a0, a2, a1], axis=1)
    rhs = jnp.concatenate([b0, b1, b0, b2, b0, b1], axis=0)
    return dot(lhs, rhs)


def invert8(cols):
    row = lax.broadcasted_iota(jnp.int32, (8, 128), 0)
    for s in range(8):
        here = row == s
        at_s = [jnp.broadcast_to(cols[q][s : s + 1, :], (8, 128)) for q in range(8)]
        inv = 1.0 / at_s[s]
        pivot = cols[s]
        fresh = []
        for q in range(8):
            if q == s:
                fresh.append(jnp.where(here, inv, -pivot * inv))
            else:
                scaled = at_s[q] * inv
                fresh.append(jnp.where(here, scaled, cols[q] - pivot * scaled))
        cols = fresh
    return cols


def spread_row(x, m):
    return jnp.broadcast_to(x[m : m + 1, :], (8, 128))


def eliminate_panel(ref, r0, depth, n):
    tiles = n // 128
    groups = depth // 8
    lane = lax.broadcasted_iota(jnp.int32, (8, 128), 1)
    row = lax.broadcasted_iota(jnp.int32, (8, 128), 0)
    x = [
        [ref[r0 + 8 * v : r0 + 8 * v + 8, 128 * t : 128 * t + 128] for t in range(tiles)]
        for v in range(groups)
    ]
    for g in range(groups):
        t_piv, l0 = divmod(r0 + 8 * g, 128)

        def column(block, q):
            return jnp.broadcast_to(block[:, l0 + q : l0 + q + 1], (8, 128))

        inv = invert8([column(x[g][t_piv], q) for q in range(8)])
        inside = (lane >= l0) & (lane < l0 + 8)
        unit = jnp.where(lane - l0 == row, 1.0, 0.0)
        fresh = []
        for t in range(tiles):
            old = x[g][t]
            if t == t_piv:
                old = jnp.where(inside, unit, old)
            y = [inv[m] * spread_row(old, m) for m in range(8)]
            fresh.append(((y[0] + y[1]) + (y[2] + y[3])) + ((y[4] + y[5]) + (y[6] + y[7])))
        for v in range(groups):
            if v == g:
                continue
            cols = [column(x[v][t_piv], m) for m in range(8)]
            for t in range(tiles):
                old = x[v][t]
                if t == t_piv:
                    old = jnp.where(inside, 0.0, old)
                y = [cols[m] * spread_row(fresh[t], m) for m in range(8)]
                x[v][t] = old - (
                    ((y[0] + y[1]) + (y[2] + y[3])) + ((y[4] + y[5]) + (y[6] + y[7]))
                )
        x[g] = fresh
    for v in range(groups):
        for t in range(tiles):
            ref[r0 + 8 * v : r0 + 8 * v + 8, 128 * t : 128 * t + 128] = x[v][t]


def invert_in_place(ref, n, depth):
    for k in range(n // depth):
        r0 = k * depth
        eliminate_panel(ref, r0, depth, n)
        panel = ref[r0 : r0 + depth, :]
        lane = lax.broadcasted_iota(jnp.int32, (1, n), 1)
        inside = (lane >= r0) & (lane < r0 + depth)
        for lo, hi in ((0, r0), (r0 + depth, n)):
            if hi > lo:
                cols = ref[lo:hi, r0 : r0 + depth]
                ref[lo:hi, :] = jnp.where(inside, 0.0, ref[lo:hi, :]) - dot_packed(cols, panel)


def coords():
    e = lax.axis_index("ep")
    t = lax.axis_index("tm")
    return e, t, t // N_X, t % N_X


def greet():
    e, t, z, x = coords()
    barrier = pltpu.get_barrier_semaphore()

    def along_tm(k, _):
        peer = lax.rem(t + k, N_TM)
        pl.semaphore_signal(barrier, inc=1, device_id=(e, peer), device_id_type=MESH)
        return 0

    def in_layer(k, _):
        pe = lax.rem(e + k // N_X, N_EP)
        px = lax.rem(x + k % N_X, N_X)
        pl.semaphore_signal(barrier, inc=1, device_id=(pe, z * N_X + px), device_id_type=MESH)
        return 0

    lax.fori_loop(1, N_TM, along_tm, 0)
    lax.fori_loop(N_X, N_EP * N_X, in_layer, 0)


def await_greetings():
    pl.semaphore_wait(pltpu.get_barrier_semaphore(), N_TM - 1 + (N_EP - 1) * N_X)


def send_tm(src_of, dst, send_sem, recv_sem):
    e, t, _, _ = coords()

    def body(k, _):
        peer = lax.rem(t + k, N_TM)
        pltpu.make_async_remote_copy(
            src_ref=src_of(peer),
            dst_ref=dst,
            send_sem=send_sem,
            recv_sem=recv_sem,
            device_id=(e, peer),
            device_id_type=MESH,
        ).start()
        return 0

    lax.fori_loop(1, N_TM, body, 0)


def send_ep(src_of, dst, send_sem, recv_sem):
    e, t, _, _ = coords()

    def body(k, _):
        peer = lax.rem(e + k, N_EP)
        pltpu.make_async_remote_copy(
            src_ref=src_of(peer),
            dst_ref=dst,
            send_sem=send_sem,
            recv_sem=recv_sem,
            device_id=(peer, t),
            device_id_type=MESH,
        ).start()
        return 0

    lax.fori_loop(1, N_EP, body, 0)


def send_layer(src, dst, send_sem, recv_sem):
    e, _, z, x = coords()

    def body(k, _):
        pe = lax.rem(e + k // N_X, N_EP)
        px = lax.rem(x + k % N_X, N_X)
        pltpu.make_async_remote_copy(
            src_ref=src,
            dst_ref=dst,
            send_sem=send_sem,
            recv_sem=recv_sem,
            device_id=(pe, z * N_X + px),
            device_id_type=MESH,
        ).start()
        return 0

    lax.fori_loop(1, N_EP * N_X, body, 0)


def settle(ref, sem):
    pltpu.make_async_copy(ref, ref, sem).wait()


def sum_slots(ref, slots, rows):
    parts = [ref[rows * s : rows * (s + 1), :] for s in range(slots)]
    while len(parts) > 1:
        parts = [parts[i] + parts[i + 1] for i in range(0, len(parts), 2)]
    return parts[0]


def rows_at(index, size):
    return pl.ds(pl.multiple_of(index * size, size), size)


def dot_t(left, right):
    return lax.dot_general(
        left, right, (((1,), (1,)), ((), ())), preferred_element_type=F32
    )


def basis_pair(b, chan_ref, k):
    return split2(jnp.concatenate([b * chan_ref[pl.ds(k + d, 1), :] for d in range(2)], axis=0))


def model_pair(acat, high, low):
    return dot_t(acat, jnp.concatenate([high, high, low], axis=1))


def pack_left(x):
    high, low = split2(x)
    return jnp.concatenate([high, low, high], axis=1)


def fit_kernel(
    obs_ref,
    miss_ref,
    a_ref,
    b_ref,
    chan_ref,
    w_ref,
    aout_ref,
    bout_ref,
    w_buf,
    miss_buf,
    xh_buf,
    xl_buf,
    a_buf,
    b_buf,
    acat,
    spread,
    gram_c,
    s_buf,
    bt_buf,
    gb_part,
    gb_recv,
    gb_full,
    me_part,
    me_recv,
    me_full,
    at_buf,
    ga_part,
    ga_recv,
    ga_full,
    mt_part,
    mt_acc,
    mt_recv,
    mt_full,
    load_sem,
    save_sem,
    send_sem,
    recv_sem,
):
    e, t, z, x = coords()
    greet()
    for g in range(N_GROUP):
        for q in range(GROUP):
            k = g * GROUP + q
            to = pl.ds(k * I_BLK, I_BLK)
            pltpu.make_async_copy(obs_ref.at[:, k, :], w_buf.at[to], load_sem.at[g]).start()
            pltpu.make_async_copy(miss_ref.at[:, k, :], miss_buf.at[to], load_sem.at[N_GROUP + g]).start()
    a_mine = rows_at(t, A_OWN)
    b_mine = rows_at(e, B_OWN)
    a_buf[a_mine, :] = a_ref[...]
    b_buf[b_mine, :] = b_ref[...]
    others_a = a_buf.at[pl.ds(0, (N_TM - 1) * A_OWN)]
    others_b = b_buf.at[pl.ds(0, (N_EP - 1) * B_OWN)]
    others_gb = gb_recv.at[pl.ds(0, (N_TM - 1) * PIECE)]
    others_gb_full = gb_full.at[pl.ds(0, (N_EP * N_X - 1) * PIECE)]
    others_me = me_recv.at[pl.ds(0, (N_TM - 1) * A_OWN)]
    others_ga = ga_recv.at[pl.ds(0, (N_EP - 1) * PIECE)]
    others_ga_full = ga_full.at[pl.ds(0, (N_EP * N_X - 1) * PIECE)]
    others_mt = mt_recv.at[pl.ds(0, (N_EP - 1) * B_OWN)]

    chan_t = chan_ref[...].T
    gram_c[...] = dot_high(chan_t, chan_ref[...])
    for g in range(N_GROUP):
        spread[g] = chan_t[:, g * GROUP : (g + 1) * GROUP]

    def mask_group(g, _):
        rows = rows_at(g, G_ROWS)
        settle(w_buf.at[rows], load_sem.at[g])
        settle(miss_buf.at[rows], load_sem.at[N_GROUP + g])

        def mask_part(q, _):
            part = rows_at(g * GROUP + q, I_BLK)
            w_buf[part, :] = jnp.where(miss_buf[part, :] == 1, jnp.nan, w_buf[part, :])
            return 0

        lax.fori_loop(0, GROUP, mask_part, 0)
        return 0

    lax.fori_loop(0, N_GROUP, mask_group, 0)
    save = pltpu.make_async_copy(w_buf, w_ref, save_sem.at[0])
    save.start()
    await_greetings()
    send_ep(lambda peer: b_buf.at[b_mine], b_buf.at[b_mine], send_sem.at[0], recv_sem.at[0])
    send_tm(lambda peer: a_buf.at[a_mine], a_buf.at[a_mine], send_sem.at[1], recv_sem.at[1])
    me_mine = rows_at(t, A_OWN)
    mt_mine = rows_at(e, B_OWN)
    others_me_full = me_full.at[pl.ds(0, (N_TM - 1) * A_OWN)]
    others_mt_full = mt_full.at[pl.ds(0, (N_EP - 1) * B_OWN)]

    def start_gram_b():
        b = b_buf[...]
        bt_buf[...] = b.T
        gb_part[...] = dot_high(bt_buf[rows_at(e, N_X * PIECE), :], b)
        gb_slot = gb_recv.at[rows_at(t, PIECE)]
        send_tm(
            lambda peer: gb_part.at[rows_at(peer % N_X, PIECE)], gb_slot, send_sem.at[2], recv_sem.at[2]
        )
        gb_recv[rows_at(t, PIECE), :] = gb_part[rows_at(x, PIECE), :]

    settle(others_b, recv_sem.at[0])
    start_gram_b()
    settle(others_a, recv_sem.at[1])
    acat[...] = pack_left(a_buf[...])
    settle(others_b, send_sem.at[0])
    settle(others_a, send_sem.at[1])

    def sweep(s, _):
        me_part[...] = jnp.zeros_like(me_part)

        def episode_group(g, _):
            for p in range(0, GROUP, 2):
                k = g * GROUP + p
                b_high, b_low = basis_pair(b_buf[...], chan_ref, k)
                model = model_pair(acat[...], b_high, b_low)
                highs, lows = [], []
                for d in range(2):
                    rows = rows_at(k + d, I_BLK)
                    w = w_buf[rows, :]
                    filled = jnp.where(w != w, model[:, d * J_BLK : (d + 1) * J_BLK], w)
                    high, low = split2(filled)
                    xh_buf[rows, :] = high
                    xl_buf[rows, :] = low
                    highs.append(high)
                    lows.append(low)
                high = jnp.concatenate(highs, axis=1)
                low = jnp.concatenate(lows, axis=1)
                me_part[...] += dot(
                    jnp.concatenate([high, low, high], axis=1),
                    jnp.concatenate([b_high, b_high, b_low], axis=0),
                )
            return 0

        lax.fori_loop(0, N_GROUP, episode_group, 0)
        me_slot = me_recv.at[rows_at(t, A_OWN)]
        send_tm(lambda peer: me_part.at[rows_at(peer, A_OWN)], me_slot, send_sem.at[4], recv_sem.at[4])
        me_recv[rows_at(t, A_OWN), :] = me_part[rows_at(t, A_OWN), :]
        settle(others_gb, recv_sem.at[2])
        gb_mine = rows_at(e * N_X + x, PIECE)
        gb_full[gb_mine, :] = sum_slots(gb_recv, N_TM, PIECE)
        send_layer(gb_full.at[gb_mine], gb_full.at[gb_mine], send_sem.at[3], recv_sem.at[3])
        settle(others_me, recv_sem.at[4])
        me_full[me_mine, :] = sum_slots(me_recv, N_TM, A_OWN)
        send_tm(lambda peer: me_full.at[me_mine], me_full.at[me_mine], send_sem.at[8], recv_sem.at[8])
        settle(others_gb_full, recv_sem.at[3])
        form_system(s_buf, gb_full, gram_c)
        invert_in_place(s_buf, RANK, 32)
        settle(others_me_full, recv_sem.at[8])
        a = dot_high(me_full[...], s_buf[...])
        a_buf[...] = a

        at = a.T
        at_buf[...] = at
        ga_part[...] = dot_high(at_buf[rows_at(x, N_EP * PIECE), :], a)
        ga_slot = ga_recv.at[rows_at(e, PIECE)]
        send_ep(lambda peer: ga_part.at[rows_at(peer, PIECE)], ga_slot, send_sem.at[5], recv_sem.at[5])
        ga_recv[rows_at(e, PIECE), :] = ga_part[rows_at(e, PIECE), :]
        acat[...] = pack_left(at_buf[...])
        settle(others_gb, send_sem.at[2])
        settle(others_gb_full, send_sem.at[3])
        settle(others_me, send_sem.at[4])
        settle(others_me_full, send_sem.at[8])
        mt_acc[...] = jnp.zeros_like(mt_acc)

        def time_group(g, _):
            for p in range(0, GROUP, 2):
                k = g * GROUP + p
                high = jnp.concatenate([xh_buf[rows_at(k + d, I_BLK), :] for d in range(2)], axis=1)
                low = jnp.concatenate([xl_buf[rows_at(k + d, I_BLK), :] for d in range(2)], axis=1)
                prod = dot(acat[...], jnp.concatenate([high, high, low], axis=0))
                terms = [
                    jnp.broadcast_to(spread[g, :, p + d : p + d + 1], (RANK, J_BLK))
                    * prod[:, d * J_BLK : (d + 1) * J_BLK]
                    for d in range(2)
                ]
                mt_acc[...] += terms[0] + terms[1]
            return 0

        lax.fori_loop(0, N_GROUP, time_group, 0)
        mt_part[...] = mt_acc[...].T
        mt_slot = mt_recv.at[rows_at(e, B_OWN)]
        send_ep(lambda peer: mt_part.at[rows_at(peer, B_OWN)], mt_slot, send_sem.at[7], recv_sem.at[7])
        mt_recv[rows_at(e, B_OWN), :] = mt_part[rows_at(e, B_OWN), :]
        settle(others_ga, recv_sem.at[5])
        ga_mine = rows_at(x * N_EP + e, PIECE)
        ga_full[ga_mine, :] = sum_slots(ga_recv, N_EP, PIECE)
        send_layer(ga_full.at[ga_mine], ga_full.at[ga_mine], send_sem.at[6], recv_sem.at[6])
        settle(others_mt, recv_sem.at[7])
        mt_full[mt_mine, :] = sum_slots(mt_recv, N_EP, B_OWN)
        send_ep(lambda peer: mt_full.at[mt_mine], mt_full.at[mt_mine], send_sem.at[9], recv_sem.at[9])
        settle(others_ga_full, recv_sem.at[6])
        form_system(s_buf, ga_full, gram_c)
        invert_in_place(s_buf, RANK, 32)
        settle(others_mt_full, recv_sem.at[9])
        b_buf[...] = dot_high(mt_full[...], s_buf[...])
        settle(others_ga, send_sem.at[5])
        settle(others_ga_full, send_sem.at[6])
        settle(others_mt, send_sem.at[7])
        settle(others_mt_full, send_sem.at[9])

        @pl.when(s < SWEEPS - 1)
        def _():
            start_gram_b()
            acat[...] = pack_left(a_buf[...])

        return 0

    lax.fori_loop(0, SWEEPS, sweep, 0)
    aout_ref[...] = a_buf[...]
    bout_ref[...] = b_buf[...]
    save.wait()


def form_system(s_ref, gram_ref, gram_c):
    eye = lax.broadcasted_iota(jnp.int32, (RANK, RANK), 0) == lax.broadcasted_iota(
        jnp.int32, (RANK, RANK), 1
    )
    s_ref[...] = gram_ref[...] * gram_c[...] + jnp.where(eye, RIDGE, 0.0)


def fit(obs, miss, a_own, b_own, channel):
    vmem = pl.BlockSpec(memory_space=pltpu.VMEM)
    anywhere = pl.BlockSpec(memory_space=pl.ANY)

    def f32(*shape):
        return pltpu.VMEM(shape, F32)

    return pl.pallas_call(
        fit_kernel,
        out_shape=(
            jax.ShapeDtypeStruct((ROWS, J_BLK), F32),
            jax.ShapeDtypeStruct((I_BLK, RANK), F32),
            jax.ShapeDtypeStruct((J_BLK, RANK), F32),
        ),
        in_specs=[anywhere, anywhere, vmem, vmem, vmem],
        out_specs=(anywhere, vmem, vmem),
        scratch_shapes=[
            f32(ROWS, J_BLK),
            pltpu.VMEM((ROWS, J_BLK), jnp.int32),
            pltpu.VMEM((ROWS, J_BLK), BF16),
            pltpu.VMEM((ROWS, J_BLK), BF16),
            f32(I_BLK, RANK),
            f32(J_BLK, RANK),
            pltpu.VMEM((I_BLK, 3 * RANK), BF16),
            f32(N_GROUP, RANK, GROUP),
            f32(RANK, RANK),
            f32(RANK, RANK),
            f32(RANK, J_BLK),
            f32(N_X * PIECE, RANK),
            f32(N_TM * PIECE, RANK),
            f32(RANK, RANK),
            f32(I_BLK, RANK),
            f32(I_BLK, RANK),
            f32(I_BLK, RANK),
            f32(RANK, I_BLK),
            f32(N_EP * PIECE, RANK),
            f32(N_EP * PIECE, RANK),
            f32(RANK, RANK),
            f32(J_BLK, RANK),
            f32(RANK, J_BLK),
            f32(J_BLK, RANK),
            f32(J_BLK, RANK),
            pltpu.SemaphoreType.DMA((2 * N_GROUP,)),
            pltpu.SemaphoreType.DMA((1,)),
            pltpu.SemaphoreType.DMA((10,)),
            pltpu.SemaphoreType.DMA((10,)),
        ],
        compiler_params=pltpu.CompilerParams(
            collective_id=0, has_side_effects=True, vmem_limit_bytes=VMEM_LIMIT
        ),
        name="fit",
    )(obs, miss, a_own, b_own, channel)


def complete_kernel(w_ref, a_ref, b_ref, chan_ref, out_ref, w_buf, acat, load_sem, save_sem):
    for g in range(N_GROUP):
        rows = pl.ds(g * G_ROWS, G_ROWS)
        pltpu.make_async_copy(w_ref.at[rows], w_buf.at[rows], load_sem.at[g]).start()
    acat[...] = pack_left(a_ref[...])

    def group(g, _):
        settle(w_buf.at[rows_at(g, G_ROWS)], load_sem.at[g])
        for p in range(0, GROUP, 2):
            k = g * GROUP + p
            b_high, b_low = basis_pair(b_ref[...], chan_ref, k)
            model = model_pair(acat[...], b_high, b_low)
            for d in range(2):
                rows = rows_at(k + d, I_BLK)
                w = w_buf[rows, :]
                w_buf[rows, :] = jnp.where(w != w, model[:, d * J_BLK : (d + 1) * J_BLK], w)
        return 0

    for g in range(N_GROUP):
        group(g, 0)
        for q in range(GROUP):
            k = g * GROUP + q
            pltpu.make_async_copy(
                w_buf.at[pl.ds(k * I_BLK, I_BLK)], out_ref.at[:, k, :], save_sem.at[g]
            ).start()
    for g in range(N_GROUP):
        settle(w_buf.at[pl.ds(g * G_ROWS, G_ROWS)], save_sem.at[g])


def complete(w, a_block, b_block, channel):
    vmem = pl.BlockSpec(memory_space=pltpu.VMEM)
    anywhere = pl.BlockSpec(memory_space=pl.ANY)
    return pl.pallas_call(
        complete_kernel,
        out_shape=jax.ShapeDtypeStruct((I_BLK, WIDTH, J_BLK), F32),
        in_specs=[anywhere, vmem, vmem, vmem],
        out_specs=anywhere,
        scratch_shapes=[
            pltpu.VMEM((ROWS, J_BLK), F32),
            pltpu.VMEM((I_BLK, 3 * RANK), BF16),
            pltpu.SemaphoreType.DMA((N_GROUP,)),
            pltpu.SemaphoreType.DMA((N_GROUP,)),
        ],
        compiler_params=pltpu.CompilerParams(vmem_limit_bytes=VMEM_LIMIT),
        name="complete",
    )(w, a_block, b_block, channel)


def on_device(observed, missing, episode_init, time_init, channel):
    obs = observed.transpose(0, 2, 1)
    miss = missing.transpose(0, 2, 1)
    w, a, b = fit(obs, miss, episode_init, time_init, channel)
    return complete(w, a, b, channel).transpose(0, 2, 1)


def solution(mesh):
    in_specs = (
        P("ep", "tm", None),
        P("ep", "tm", None),
        P(("ep", "tm"), None),
        P(("tm", "ep"), None),
        P(),
    )
    return jax.shard_map(
        on_device, mesh=mesh, in_specs=in_specs, out_specs=P("ep", "tm", None), check_vma=False
    )
```

```python
import jax
import jax.numpy as jnp
from jax import lax
from jax.experimental import pallas as pl
from jax.experimental.pallas import tpu as pltpu
from jax.sharding import PartitionSpec as P

SWEEPS = 2
RIDGE = 1.0
HIGH = lax.Precision.HIGHEST
F32 = jnp.float32
BF16 = jnp.bfloat16
MESH = pl.DeviceIdType.MESH

RANK = 256
WIDTH = 32
N_EP = 8
N_TM = 32
N_X = 4
I_BLK = 256
J_BLK = 128
ROWS = I_BLK * WIDTH
GROUP = 8
N_GROUP = WIDTH // GROUP
G_ROWS = GROUP * I_BLK
A_OWN = 8
B_OWN = 16
PIECE = 8
HALF = 128
PANEL = 32
N_PIECE = N_EP * N_X
VMEM_LIMIT = 56 * 1024 * 1024


def dot(left, right):
    return lax.dot_general(
        left, right, (((1,), (0,)), ((), ())), preferred_element_type=F32
    )


def dot_high(left, right):
    return lax.dot_general(
        left, right, (((1,), (0,)), ((), ())), precision=HIGH, preferred_element_type=F32
    )


def split2(x):
    high = x.astype(BF16)
    return high, (x - high.astype(F32)).astype(BF16)


def split3(x):
    high = x.astype(BF16)
    rest = x - high.astype(F32)
    mid = rest.astype(BF16)
    return high, mid, (rest - mid.astype(F32)).astype(BF16)


def dot_packed(left, right):
    a0, a1, a2 = split3(left)
    b0, b1, b2 = split3(right)
    lhs = jnp.concatenate([a0, a0, a1, a0, a2, a1], axis=1)
    rhs = jnp.concatenate([b0, b1, b0, b2, b0, b1], axis=0)
    return dot(lhs, rhs)


def invert8(cols):
    row = lax.broadcasted_iota(jnp.int32, (8, 128), 0)
    for s in range(8):
        here = row == s
        at_s = [jnp.broadcast_to(cols[q][s : s + 1, :], (8, 128)) for q in range(8)]
        inv = 1.0 / at_s[s]
        pivot = cols[s]
        fresh = []
        for q in range(8):
            if q == s:
                fresh.append(jnp.where(here, inv, -pivot * inv))
            else:
                scaled = at_s[q] * inv
                fresh.append(jnp.where(here, scaled, cols[q] - pivot * scaled))
        cols = fresh
    return cols


def spread_row(x, m):
    return jnp.broadcast_to(x[m : m + 1, :], (8, 128))


def eliminate_panel(ref, r0, depth, n):
    tiles = n // 128
    groups = depth // 8
    lane = lax.broadcasted_iota(jnp.int32, (8, 128), 1)
    row = lax.broadcasted_iota(jnp.int32, (8, 128), 0)
    x = [
        [ref[r0 + 8 * v : r0 + 8 * v + 8, 128 * t : 128 * t + 128] for t in range(tiles)]
        for v in range(groups)
    ]
    for g in range(groups):
        t_piv, l0 = divmod(r0 + 8 * g, 128)

        def column(block, q):
            return jnp.broadcast_to(block[:, l0 + q : l0 + q + 1], (8, 128))

        inv = invert8([column(x[g][t_piv], q) for q in range(8)])
        inside = (lane >= l0) & (lane < l0 + 8)
        unit = jnp.where(lane - l0 == row, 1.0, 0.0)
        fresh = []
        for t in range(tiles):
            old = x[g][t]
            if t == t_piv:
                old = jnp.where(inside, unit, old)
            y = [inv[m] * spread_row(old, m) for m in range(8)]
            fresh.append(((y[0] + y[1]) + (y[2] + y[3])) + ((y[4] + y[5]) + (y[6] + y[7])))
        for v in range(groups):
            if v == g:
                continue
            cols = [column(x[v][t_piv], m) for m in range(8)]
            for t in range(tiles):
                old = x[v][t]
                if t == t_piv:
                    old = jnp.where(inside, 0.0, old)
                y = [cols[m] * spread_row(fresh[t], m) for m in range(8)]
                x[v][t] = old - (
                    ((y[0] + y[1]) + (y[2] + y[3])) + ((y[4] + y[5]) + (y[6] + y[7]))
                )
        x[g] = fresh
    for v in range(groups):
        for t in range(tiles):
            ref[r0 + 8 * v : r0 + 8 * v + 8, 128 * t : 128 * t + 128] = x[v][t]


def eliminate_rows(ref, lo, hi, r0, depth):
    n = ref.shape[1]
    lane = lax.broadcasted_iota(jnp.int32, (1, n), 1)
    inside = (lane >= r0) & (lane < r0 + depth)
    product = dot_packed(ref[lo:hi, r0 : r0 + depth], ref[r0 : r0 + depth, :])
    ref[lo:hi, :] = jnp.where(inside, 0.0, ref[lo:hi, :]) - product


def eliminate_half(ref, base, depth, between=None):
    top = base + HALF
    for r0 in range(base, top, depth):
        eliminate_panel(ref, r0, depth, ref.shape[1])
        for lo, hi in ((base, r0), (r0 + depth, top)):
            if hi > lo:
                eliminate_rows(ref, lo, hi, r0, depth)
        if between is not None and r0 == base + depth:
            between()


def coords():
    e = lax.axis_index("ep")
    t = lax.axis_index("tm")
    return e, t, t // N_X, t % N_X


def greet():
    e, t, z, x = coords()
    barrier = pltpu.get_barrier_semaphore()

    def along_tm(k, _):
        peer = lax.rem(t + k, N_TM)
        pl.semaphore_signal(barrier, inc=1, device_id=(e, peer), device_id_type=MESH)
        return 0

    def in_layer(k, _):
        pe = lax.rem(e + k // N_X, N_EP)
        px = lax.rem(x + k % N_X, N_X)
        pl.semaphore_signal(barrier, inc=1, device_id=(pe, z * N_X + px), device_id_type=MESH)
        return 0

    lax.fori_loop(1, N_TM, along_tm, 0)
    lax.fori_loop(N_X, N_EP * N_X, in_layer, 0)


def await_greetings():
    pl.semaphore_wait(pltpu.get_barrier_semaphore(), N_TM - 1 + (N_EP - 1) * N_X)


def send_tm(src_of, dst, send_sem, recv_sem):
    e, t, _, _ = coords()

    def body(k, _):
        peer = lax.rem(t + k, N_TM)
        pltpu.make_async_remote_copy(
            src_ref=src_of(peer),
            dst_ref=dst,
            send_sem=send_sem,
            recv_sem=recv_sem,
            device_id=(e, peer),
            device_id_type=MESH,
        ).start()
        return 0

    lax.fori_loop(1, N_TM, body, 0)


def send_ep(src_of, dst, send_sem, recv_sem):
    e, t, _, _ = coords()

    def body(k, _):
        peer = lax.rem(e + k, N_EP)
        pltpu.make_async_remote_copy(
            src_ref=src_of(peer),
            dst_ref=dst,
            send_sem=send_sem,
            recv_sem=recv_sem,
            device_id=(peer, t),
            device_id_type=MESH,
        ).start()
        return 0

    lax.fori_loop(1, N_EP, body, 0)


def send_layer(src, dst, send_sem, recv_sem):
    e, _, z, x = coords()

    def body(k, _):
        pe = lax.rem(e + k // N_X, N_EP)
        px = lax.rem(x + k % N_X, N_X)
        pltpu.make_async_remote_copy(
            src_ref=src,
            dst_ref=dst,
            send_sem=send_sem,
            recv_sem=recv_sem,
            device_id=(pe, z * N_X + px),
            device_id_type=MESH,
        ).start()
        return 0

    lax.fori_loop(1, N_EP * N_X, body, 0)


def settle(ref, sem):
    pltpu.make_async_copy(ref, ref, sem).wait()


def sum_slots(ref, slots, rows):
    parts = [ref[rows * s : rows * (s + 1), :] for s in range(slots)]
    while len(parts) > 1:
        parts = [parts[i] + parts[i + 1] for i in range(0, len(parts), 2)]
    return parts[0]


def rows_at(index, size):
    return pl.ds(pl.multiple_of(index * size, size), size)


def dot_t(left, right):
    return lax.dot_general(
        left, right, (((1,), (1,)), ((), ())), preferred_element_type=F32
    )


def basis_pair(b, chan_ref, k):
    return split2(jnp.concatenate([b * chan_ref[pl.ds(k + d, 1), :] for d in range(2)], axis=0))


def model_pair(acat, high, low):
    return dot_t(acat, jnp.concatenate([high, high, low], axis=1))


def pack_left(x):
    high, low = split2(x)
    return jnp.concatenate([high, low, high], axis=1)


def fit_kernel(
    obs_ref,
    miss_ref,
    a_ref,
    b_ref,
    chan_ref,
    w_ref,
    aout_ref,
    bout_ref,
    w_buf,
    miss_buf,
    xh_buf,
    xl_buf,
    a_buf,
    b_buf,
    acat,
    spread,
    gram_c,
    s_buf,
    bt_buf,
    gb_part,
    gb_recv,
    gb_full,
    me_part,
    me_recv,
    me_full,
    at_buf,
    ga_part,
    ga_recv,
    ga_full,
    mt_part,
    mt_acc,
    mt_recv,
    mt_full,
    load_sem,
    save_sem,
    send_sem,
    recv_sem,
):
    e, t, z, x = coords()
    greet()
    for g in range(N_GROUP):
        for q in range(GROUP):
            k = g * GROUP + q
            to = pl.ds(k * I_BLK, I_BLK)
            pltpu.make_async_copy(obs_ref.at[:, k, :], w_buf.at[to], load_sem.at[g]).start()
            pltpu.make_async_copy(miss_ref.at[:, k, :], miss_buf.at[to], load_sem.at[N_GROUP + g]).start()
    a_mine = rows_at(t, A_OWN)
    b_mine = rows_at(e, B_OWN)
    a_buf[a_mine, :] = a_ref[...]
    b_buf[b_mine, :] = b_ref[...]
    others_a = a_buf.at[pl.ds(0, (N_TM - 1) * A_OWN)]
    others_b = b_buf.at[pl.ds(0, (N_EP - 1) * B_OWN)]
    others_gb = [gb_recv.at[h, pl.ds(0, (N_TM - 1) * PIECE)] for h in range(2)]
    others_gb_full = [gb_full.at[h, pl.ds(0, (N_PIECE - 1) * PIECE)] for h in range(2)]
    others_me = me_recv.at[pl.ds(0, (N_TM - 1) * A_OWN)]
    others_ga = [ga_recv.at[h, pl.ds(0, (N_EP - 1) * PIECE)] for h in range(2)]
    others_ga_full = [ga_full.at[h, pl.ds(0, (N_PIECE - 1) * PIECE)] for h in range(2)]
    others_mt = mt_recv.at[pl.ds(0, (N_EP - 1) * B_OWN)]

    chan_t = chan_ref[...].T
    gram_c[...] = dot_high(chan_t, chan_ref[...])
    for g in range(N_GROUP):
        spread[g] = chan_t[:, g * GROUP : (g + 1) * GROUP]

    def mask_group(g, _):
        rows = rows_at(g, G_ROWS)
        settle(w_buf.at[rows], load_sem.at[g])
        settle(miss_buf.at[rows], load_sem.at[N_GROUP + g])

        def mask_part(q, _):
            part = rows_at(g * GROUP + q, I_BLK)
            w_buf[part, :] = jnp.where(miss_buf[part, :] == 1, jnp.nan, w_buf[part, :])
            return 0

        lax.fori_loop(0, GROUP, mask_part, 0)
        return 0

    lax.fori_loop(0, N_GROUP, mask_group, 0)
    save = pltpu.make_async_copy(w_buf, w_ref, save_sem.at[0])
    save.start()
    await_greetings()
    send_ep(lambda peer: b_buf.at[b_mine], b_buf.at[b_mine], send_sem.at[0], recv_sem.at[0])
    send_tm(lambda peer: a_buf.at[a_mine], a_buf.at[a_mine], send_sem.at[1], recv_sem.at[1])
    me_mine = rows_at(t, A_OWN)
    mt_mine = rows_at(e, B_OWN)
    others_me_full = me_full.at[pl.ds(0, (N_TM - 1) * A_OWN)]
    others_mt_full = mt_full.at[pl.ds(0, (N_EP - 1) * B_OWN)]

    def start_gram_b():
        b = b_buf[...]
        bt_buf[...] = b.T
        for h in range(2):
            slab = pl.ds(pl.multiple_of(h * HALF + e * 2 * PIECE, PIECE), 2 * PIECE)
            store_pieces(gb_part, h, dot_high(bt_buf[slab, :], b))
            send_tm(
                lambda peer: gb_part.at[h, rows_at(peer % N_X, PIECE)],
                gb_recv.at[h, rows_at(t, PIECE)],
                send_sem.at[2 + h],
                recv_sem.at[2 + h],
            )
            gb_recv[h, rows_at(t, PIECE), :] = gb_part[h, rows_at(x, PIECE), :]

    settle(others_b, recv_sem.at[0])
    start_gram_b()
    settle(others_a, recv_sem.at[1])
    acat[...] = pack_left(a_buf[...])
    settle(others_b, send_sem.at[0])
    settle(others_a, send_sem.at[1])

    def sweep(s, _):
        me_part[...] = jnp.zeros_like(me_part)

        def episode_group(g, _):
            for p in range(0, GROUP, 2):
                k = g * GROUP + p
                b_high, b_low = basis_pair(b_buf[...], chan_ref, k)
                model = model_pair(acat[...], b_high, b_low)
                highs, lows = [], []
                for d in range(2):
                    rows = rows_at(k + d, I_BLK)
                    w = w_buf[rows, :]
                    filled = jnp.where(w != w, model[:, d * J_BLK : (d + 1) * J_BLK], w)
                    high, low = split2(filled)
                    xh_buf[rows, :] = high
                    xl_buf[rows, :] = low
                    highs.append(high)
                    lows.append(low)
                high = jnp.concatenate(highs, axis=1)
                low = jnp.concatenate(lows, axis=1)
                me_part[...] += dot(
                    jnp.concatenate([high, low, high], axis=1),
                    jnp.concatenate([b_high, b_high, b_low], axis=0),
                )
            return 0

        lax.fori_loop(0, N_GROUP, episode_group, 0)
        me_slot = me_recv.at[rows_at(t, A_OWN)]
        send_tm(lambda peer: me_part.at[rows_at(peer, A_OWN)], me_slot, send_sem.at[6], recv_sem.at[6])
        me_recv[rows_at(t, A_OWN), :] = me_part[rows_at(t, A_OWN), :]
        gb_mine = rows_at(e * N_X + x, PIECE)
        for h in range(2):
            settle(others_gb[h], recv_sem.at[2 + h])
            gb_full[h, gb_mine, :] = sum_slots(gb_recv.at[h], N_TM, PIECE)
            mine = gb_full.at[h, gb_mine]
            send_layer(mine, mine, send_sem.at[4 + h], recv_sem.at[4 + h])
        settle(others_gb_full[0], recv_sem.at[4])
        form_half(s_buf, gb_full, gram_c, 0)

        def share_me():
            settle(others_me, recv_sem.at[6])
            me_full[me_mine, :] = sum_slots(me_recv, N_TM, A_OWN)
            mine = me_full.at[me_mine]
            send_tm(lambda peer: mine, mine, send_sem.at[7], recv_sem.at[7])

        eliminate_half(s_buf, 0, PANEL, share_me)
        settle(others_gb_full[1], recv_sem.at[5])
        form_half(s_buf, gb_full, gram_c, 1)
        finish_inverse(s_buf)
        settle(others_me_full, recv_sem.at[7])
        a = dot_high(me_full[...], s_buf[...])
        a_buf[...] = a

        at = a.T
        at_buf[...] = at
        for h in range(2):
            slab = pl.ds(pl.multiple_of(h * HALF + x * 4 * PIECE, PIECE), 4 * PIECE)
            store_pieces(ga_part, h, dot_high(at_buf[slab, :], a))
            send_ep(
                lambda peer: ga_part.at[h, rows_at(peer, PIECE)],
                ga_recv.at[h, rows_at(e, PIECE)],
                send_sem.at[8 + h],
                recv_sem.at[8 + h],
            )
            ga_recv[h, rows_at(e, PIECE), :] = ga_part[h, rows_at(e, PIECE), :]
        acat[...] = pack_left(at_buf[...])
        for h in range(2):
            settle(others_gb[h], send_sem.at[2 + h])
            settle(others_gb_full[h], send_sem.at[4 + h])
        settle(others_me, send_sem.at[6])
        settle(others_me_full, send_sem.at[7])
        mt_acc[...] = jnp.zeros_like(mt_acc)

        def time_group(g, _):
            for p in range(0, GROUP, 2):
                k = g * GROUP + p
                high = jnp.concatenate([xh_buf[rows_at(k + d, I_BLK), :] for d in range(2)], axis=1)
                low = jnp.concatenate([xl_buf[rows_at(k + d, I_BLK), :] for d in range(2)], axis=1)
                prod = dot(acat[...], jnp.concatenate([high, high, low], axis=0))
                terms = [
                    jnp.broadcast_to(spread[g, :, p + d : p + d + 1], (RANK, J_BLK))
                    * prod[:, d * J_BLK : (d + 1) * J_BLK]
                    for d in range(2)
                ]
                mt_acc[...] += terms[0] + terms[1]
            return 0

        lax.fori_loop(0, N_GROUP, time_group, 0)
        mt_part[...] = mt_acc[...].T
        mt_slot = mt_recv.at[rows_at(e, B_OWN)]
        send_ep(lambda peer: mt_part.at[rows_at(peer, B_OWN)], mt_slot, send_sem.at[12], recv_sem.at[12])
        mt_recv[rows_at(e, B_OWN), :] = mt_part[rows_at(e, B_OWN), :]
        ga_mine = rows_at(x * N_EP + e, PIECE)
        for h in range(2):
            settle(others_ga[h], recv_sem.at[8 + h])
            ga_full[h, ga_mine, :] = sum_slots(ga_recv.at[h], N_EP, PIECE)
            mine = ga_full.at[h, ga_mine]
            send_layer(mine, mine, send_sem.at[10 + h], recv_sem.at[10 + h])
        settle(others_mt, recv_sem.at[12])
        mt_full[mt_mine, :] = sum_slots(mt_recv, N_EP, B_OWN)
        send_ep(lambda peer: mt_full.at[mt_mine], mt_full.at[mt_mine], send_sem.at[13], recv_sem.at[13])
        settle(others_ga_full[0], recv_sem.at[10])
        form_half(s_buf, ga_full, gram_c, 0)
        eliminate_half(s_buf, 0, PANEL)
        settle(others_ga_full[1], recv_sem.at[11])
        form_half(s_buf, ga_full, gram_c, 1)
        finish_inverse(s_buf)
        settle(others_mt_full, recv_sem.at[13])
        b_buf[...] = dot_high(mt_full[...], s_buf[...])
        for h in range(2):
            settle(others_ga[h], send_sem.at[8 + h])
            settle(others_ga_full[h], send_sem.at[10 + h])
        settle(others_mt, send_sem.at[12])
        settle(others_mt_full, send_sem.at[13])

        @pl.when(s < SWEEPS - 1)
        def _():
            start_gram_b()
            acat[...] = pack_left(a_buf[...])

        return 0

    lax.fori_loop(0, SWEEPS, sweep, 0)
    aout_ref[...] = a_buf[...]
    bout_ref[...] = b_buf[...]
    save.wait()


def store_pieces(ref, h, rows):
    for p in range(2 * rows.shape[0] // PIECE):
        r, c = PIECE * (p // 2), HALF * (p % 2)
        ref[h, PIECE * p : PIECE * (p + 1), :] = rows[r : r + PIECE, c : c + HALF]


def form_half(s_ref, gram_ref, gram_c, h):
    row = lax.broadcasted_iota(jnp.int32, (PIECE, HALF), 0)
    lane = lax.broadcasted_iota(jnp.int32, (PIECE, HALF), 1)
    for p in range(N_PIECE):
        r, c = h * HALF + PIECE * (p // 2), HALF * (p % 2)
        part = gram_ref[h, PIECE * p : PIECE * (p + 1), :] * gram_c[r : r + PIECE, c : c + HALF]
        s_ref[r : r + PIECE, c : c + HALF] = part + jnp.where(row + r == lane + c, RIDGE, 0.0)


def finish_inverse(s_ref):
    eliminate_rows(s_ref, HALF, RANK, 0, HALF)
    eliminate_half(s_ref, HALF, PANEL)
    eliminate_rows(s_ref, 0, HALF, HALF, HALF)


def fit(obs, miss, a_own, b_own, channel):
    vmem = pl.BlockSpec(memory_space=pltpu.VMEM)
    anywhere = pl.BlockSpec(memory_space=pl.ANY)

    def f32(*shape):
        return pltpu.VMEM(shape, F32)

    return pl.pallas_call(
        fit_kernel,
        out_shape=(
            jax.ShapeDtypeStruct((ROWS, J_BLK), F32),
            jax.ShapeDtypeStruct((I_BLK, RANK), F32),
            jax.ShapeDtypeStruct((J_BLK, RANK), F32),
        ),
        in_specs=[anywhere, anywhere, vmem, vmem, vmem],
        out_specs=(anywhere, vmem, vmem),
        scratch_shapes=[
            f32(ROWS, J_BLK),
            pltpu.VMEM((ROWS, J_BLK), jnp.int32),
            pltpu.VMEM((ROWS, J_BLK), BF16),
            pltpu.VMEM((ROWS, J_BLK), BF16),
            f32(I_BLK, RANK),
            f32(J_BLK, RANK),
            pltpu.VMEM((I_BLK, 3 * RANK), BF16),
            f32(N_GROUP, RANK, GROUP),
            f32(RANK, RANK),
            f32(RANK, RANK),
            f32(RANK, J_BLK),
            f32(2, N_X * PIECE, HALF),
            f32(2, N_TM * PIECE, HALF),
            f32(2, N_PIECE * PIECE, HALF),
            f32(I_BLK, RANK),
            f32(I_BLK, RANK),
            f32(I_BLK, RANK),
            f32(RANK, I_BLK),
            f32(2, N_EP * PIECE, HALF),
            f32(2, N_EP * PIECE, HALF),
            f32(2, N_PIECE * PIECE, HALF),
            f32(J_BLK, RANK),
            f32(RANK, J_BLK),
            f32(J_BLK, RANK),
            f32(J_BLK, RANK),
            pltpu.SemaphoreType.DMA((2 * N_GROUP,)),
            pltpu.SemaphoreType.DMA((1,)),
            pltpu.SemaphoreType.DMA((14,)),
            pltpu.SemaphoreType.DMA((14,)),
        ],
        compiler_params=pltpu.CompilerParams(
            collective_id=0, has_side_effects=True, vmem_limit_bytes=VMEM_LIMIT
        ),
        name="fit",
    )(obs, miss, a_own, b_own, channel)


def complete_kernel(w_ref, a_ref, b_ref, chan_ref, out_ref, w_buf, acat, load_sem, save_sem):
    for g in range(N_GROUP):
        rows = pl.ds(g * G_ROWS, G_ROWS)
        pltpu.make_async_copy(w_ref.at[rows], w_buf.at[rows], load_sem.at[g]).start()
    acat[...] = pack_left(a_ref[...])

    def group(g, _):
        settle(w_buf.at[rows_at(g, G_ROWS)], load_sem.at[g])
        for p in range(0, GROUP, 2):
            k = g * GROUP + p
            b_high, b_low = basis_pair(b_ref[...], chan_ref, k)
            model = model_pair(acat[...], b_high, b_low)
            for d in range(2):
                rows = rows_at(k + d, I_BLK)
                w = w_buf[rows, :]
                w_buf[rows, :] = jnp.where(w != w, model[:, d * J_BLK : (d + 1) * J_BLK], w)
        return 0

    for g in range(N_GROUP):
        group(g, 0)
        for q in range(GROUP):
            k = g * GROUP + q
            pltpu.make_async_copy(
                w_buf.at[pl.ds(k * I_BLK, I_BLK)], out_ref.at[:, k, :], save_sem.at[g]
            ).start()
    for g in range(N_GROUP):
        settle(w_buf.at[pl.ds(g * G_ROWS, G_ROWS)], save_sem.at[g])


def complete(w, a_block, b_block, channel):
    vmem = pl.BlockSpec(memory_space=pltpu.VMEM)
    anywhere = pl.BlockSpec(memory_space=pl.ANY)
    return pl.pallas_call(
        complete_kernel,
        out_shape=jax.ShapeDtypeStruct((I_BLK, WIDTH, J_BLK), F32),
        in_specs=[anywhere, vmem, vmem, vmem],
        out_specs=anywhere,
        scratch_shapes=[
            pltpu.VMEM((ROWS, J_BLK), F32),
            pltpu.VMEM((I_BLK, 3 * RANK), BF16),
            pltpu.SemaphoreType.DMA((N_GROUP,)),
            pltpu.SemaphoreType.DMA((N_GROUP,)),
        ],
        compiler_params=pltpu.CompilerParams(vmem_limit_bytes=VMEM_LIMIT),
        name="complete",
    )(w, a_block, b_block, channel)


def on_device(observed, missing, episode_init, time_init, channel):
    obs = observed.transpose(0, 2, 1)
    miss = missing.transpose(0, 2, 1)
    w, a, b = fit(obs, miss, episode_init, time_init, channel)
    return complete(w, a, b, channel).transpose(0, 2, 1)


def solution(mesh):
    in_specs = (
        P("ep", "tm", None),
        P("ep", "tm", None),
        P(("ep", "tm"), None),
        P(("tm", "ep"), None),
        P(),
    )
    return jax.shard_map(
        on_device, mesh=mesh, in_specs=in_specs, out_specs=P("ep", "tm", None), check_vma=False
    )
```

```python
import jax
import jax.numpy as jnp
from jax import lax
from jax.experimental import pallas as pl
from jax.experimental.pallas import tpu as pltpu
from jax.sharding import PartitionSpec as P

SWEEPS = 2
RIDGE = 1.0
HIGH = lax.Precision.HIGHEST
F32 = jnp.float32
BF16 = jnp.bfloat16
MESH = pl.DeviceIdType.MESH

RANK = 256
WIDTH = 32
N_EP = 8
N_TM = 32
N_X = 4
I_BLK = 256
J_BLK = 128
ROWS = I_BLK * WIDTH
GROUP = 8
N_GROUP = WIDTH // GROUP
G_ROWS = GROUP * I_BLK
A_OWN = 8
B_OWN = 16
PIECE = 8
HALF = 128
PANEL = 16
N_PIECE = N_EP * N_X
VMEM_LIMIT = 56 * 1024 * 1024


def dot(left, right):
    return lax.dot_general(
        left, right, (((1,), (0,)), ((), ())), preferred_element_type=F32
    )


def dot_high(left, right):
    return lax.dot_general(
        left, right, (((1,), (0,)), ((), ())), precision=HIGH, preferred_element_type=F32
    )


def split2(x):
    high = x.astype(BF16)
    return high, (x - high.astype(F32)).astype(BF16)


def split3(x):
    high = x.astype(BF16)
    rest = x - high.astype(F32)
    mid = rest.astype(BF16)
    return high, mid, (rest - mid.astype(F32)).astype(BF16)


def dot_packed(left, right):
    a0, a1, a2 = split3(left)
    b0, b1, b2 = split3(right)
    lhs = jnp.concatenate([a0, a0, a1, a0, a2, a1], axis=1)
    rhs = jnp.concatenate([b0, b1, b0, b2, b0, b1], axis=0)
    return dot(lhs, rhs)


def invert8(cols):
    row = lax.broadcasted_iota(jnp.int32, (8, 128), 0)
    for s in range(8):
        here = row == s
        at_s = [jnp.broadcast_to(cols[q][s : s + 1, :], (8, 128)) for q in range(8)]
        inv = 1.0 / at_s[s]
        pivot = cols[s]
        fresh = []
        for q in range(8):
            if q == s:
                fresh.append(jnp.where(here, inv, -pivot * inv))
            else:
                scaled = at_s[q] * inv
                fresh.append(jnp.where(here, scaled, cols[q] - pivot * scaled))
        cols = fresh
    return cols


def spread_row(x, m):
    return jnp.broadcast_to(x[m : m + 1, :], (8, 128))


def eliminate_panel(ref, r0, depth, n):
    tiles = n // 128
    groups = depth // 8
    lane = lax.broadcasted_iota(jnp.int32, (8, 128), 1)
    row = lax.broadcasted_iota(jnp.int32, (8, 128), 0)
    x = [
        [ref[r0 + 8 * v : r0 + 8 * v + 8, 128 * t : 128 * t + 128] for t in range(tiles)]
        for v in range(groups)
    ]
    for g in range(groups):
        t_piv, l0 = divmod(r0 + 8 * g, 128)

        def column(block, q):
            return jnp.broadcast_to(block[:, l0 + q : l0 + q + 1], (8, 128))

        inv = invert8([column(x[g][t_piv], q) for q in range(8)])
        inside = (lane >= l0) & (lane < l0 + 8)
        unit = jnp.where(lane - l0 == row, 1.0, 0.0)
        fresh = []
        for t in range(tiles):
            old = x[g][t]
            if t == t_piv:
                old = jnp.where(inside, unit, old)
            y = [inv[m] * spread_row(old, m) for m in range(8)]
            fresh.append(((y[0] + y[1]) + (y[2] + y[3])) + ((y[4] + y[5]) + (y[6] + y[7])))
        for v in range(groups):
            if v == g:
                continue
            cols = [column(x[v][t_piv], m) for m in range(8)]
            for t in range(tiles):
                old = x[v][t]
                if t == t_piv:
                    old = jnp.where(inside, 0.0, old)
                y = [cols[m] * spread_row(fresh[t], m) for m in range(8)]
                x[v][t] = old - (
                    ((y[0] + y[1]) + (y[2] + y[3])) + ((y[4] + y[5]) + (y[6] + y[7]))
                )
        x[g] = fresh
    for v in range(groups):
        for t in range(tiles):
            ref[r0 + 8 * v : r0 + 8 * v + 8, 128 * t : 128 * t + 128] = x[v][t]


def eliminate_rows(ref, lo, hi, r0, depth):
    n = ref.shape[1]
    lane = lax.broadcasted_iota(jnp.int32, (1, n), 1)
    inside = (lane >= r0) & (lane < r0 + depth)
    product = dot_packed(ref[lo:hi, r0 : r0 + depth], ref[r0 : r0 + depth, :])
    ref[lo:hi, :] = jnp.where(inside, 0.0, ref[lo:hi, :]) - product


def eliminate_half(ref, base, depth, between=None):
    top = base + HALF
    for r0 in range(base, top, depth):
        eliminate_panel(ref, r0, depth, ref.shape[1])
        for lo, hi in ((base, r0), (r0 + depth, top)):
            if hi > lo:
                eliminate_rows(ref, lo, hi, r0, depth)
        if between is not None and r0 == base + 3 * depth:
            between()


def coords():
    e = lax.axis_index("ep")
    t = lax.axis_index("tm")
    return e, t, t // N_X, t % N_X


def greet():
    e, t, z, x = coords()
    barrier = pltpu.get_barrier_semaphore()

    def along_tm(k, _):
        peer = lax.rem(t + k, N_TM)
        pl.semaphore_signal(barrier, inc=1, device_id=(e, peer), device_id_type=MESH)
        return 0

    def in_layer(k, _):
        pe = lax.rem(e + k // N_X, N_EP)
        px = lax.rem(x + k % N_X, N_X)
        pl.semaphore_signal(barrier, inc=1, device_id=(pe, z * N_X + px), device_id_type=MESH)
        return 0

    lax.fori_loop(1, N_TM, along_tm, 0)
    lax.fori_loop(N_X, N_EP * N_X, in_layer, 0)


def await_greetings():
    pl.semaphore_wait(pltpu.get_barrier_semaphore(), N_TM - 1 + (N_EP - 1) * N_X)


def send_tm(src_of, dst, send_sem, recv_sem):
    e, t, _, _ = coords()

    def body(k, _):
        peer = lax.rem(t + k, N_TM)
        pltpu.make_async_remote_copy(
            src_ref=src_of(peer),
            dst_ref=dst,
            send_sem=send_sem,
            recv_sem=recv_sem,
            device_id=(e, peer),
            device_id_type=MESH,
        ).start()
        return 0

    lax.fori_loop(1, N_TM, body, 0)


def send_ep(src_of, dst, send_sem, recv_sem):
    e, t, _, _ = coords()

    def body(k, _):
        peer = lax.rem(e + k, N_EP)
        pltpu.make_async_remote_copy(
            src_ref=src_of(peer),
            dst_ref=dst,
            send_sem=send_sem,
            recv_sem=recv_sem,
            device_id=(peer, t),
            device_id_type=MESH,
        ).start()
        return 0

    lax.fori_loop(1, N_EP, body, 0)


def send_layer(src, dst, send_sem, recv_sem):
    e, _, z, x = coords()

    def body(k, _):
        pe = lax.rem(e + k // N_X, N_EP)
        px = lax.rem(x + k % N_X, N_X)
        pltpu.make_async_remote_copy(
            src_ref=src,
            dst_ref=dst,
            send_sem=send_sem,
            recv_sem=recv_sem,
            device_id=(pe, z * N_X + px),
            device_id_type=MESH,
        ).start()
        return 0

    lax.fori_loop(1, N_EP * N_X, body, 0)


def settle(ref, sem):
    pltpu.make_async_copy(ref, ref, sem).wait()


def sum_slots(ref, slots, rows):
    parts = [ref[rows * s : rows * (s + 1), :] for s in range(slots)]
    while len(parts) > 1:
        parts = [parts[i] + parts[i + 1] for i in range(0, len(parts), 2)]
    return parts[0]


def rows_at(index, size):
    return pl.ds(pl.multiple_of(index * size, size), size)


def dot_t(left, right):
    return lax.dot_general(
        left, right, (((1,), (1,)), ((), ())), preferred_element_type=F32
    )


def basis_pair(b, chan_ref, k):
    return split2(jnp.concatenate([b * chan_ref[pl.ds(k + d, 1), :] for d in range(2)], axis=0))


def model_pair(acat, high, low):
    return dot_t(acat, jnp.concatenate([high, high, low], axis=1))


def pack_left(x):
    high, low = split2(x)
    return jnp.concatenate([high, low, high], axis=1)


def fit_kernel(
    obs_ref,
    miss_ref,
    a_ref,
    b_ref,
    chan_ref,
    w_ref,
    aout_ref,
    bout_ref,
    w_buf,
    miss_buf,
    xh_buf,
    xl_buf,
    a_buf,
    b_buf,
    acat,
    spread,
    gram_c,
    s_buf,
    bt_buf,
    gb_part,
    gb_recv,
    gb_full,
    me_part,
    me_recv,
    me_full,
    at_buf,
    ga_part,
    ga_recv,
    ga_full,
    mt_part,
    mt_acc,
    mt_recv,
    mt_full,
    load_sem,
    save_sem,
    send_sem,
    recv_sem,
):
    e, t, z, x = coords()
    greet()
    for g in range(N_GROUP):
        for q in range(GROUP):
            k = g * GROUP + q
            to = pl.ds(k * I_BLK, I_BLK)
            pltpu.make_async_copy(obs_ref.at[:, k, :], w_buf.at[to], load_sem.at[g]).start()
            pltpu.make_async_copy(miss_ref.at[:, k, :], miss_buf.at[to], load_sem.at[N_GROUP + g]).start()
    a_mine = rows_at(t, A_OWN)
    b_mine = rows_at(e, B_OWN)
    a_buf[a_mine, :] = a_ref[...]
    b_buf[b_mine, :] = b_ref[...]
    others_a = a_buf.at[pl.ds(0, (N_TM - 1) * A_OWN)]
    others_b = b_buf.at[pl.ds(0, (N_EP - 1) * B_OWN)]
    others_gb = [gb_recv.at[h, pl.ds(0, (N_TM - 1) * PIECE)] for h in range(2)]
    others_gb_full = [gb_full.at[h, pl.ds(0, (N_PIECE - 1) * PIECE)] for h in range(2)]
    others_me = me_recv.at[pl.ds(0, (N_TM - 1) * A_OWN)]
    others_ga = [ga_recv.at[h, pl.ds(0, (N_EP - 1) * PIECE)] for h in range(2)]
    others_ga_full = [ga_full.at[h, pl.ds(0, (N_PIECE - 1) * PIECE)] for h in range(2)]
    others_mt = mt_recv.at[pl.ds(0, (N_EP - 1) * B_OWN)]

    chan_t = chan_ref[...].T
    gram_c[...] = dot_high(chan_t, chan_ref[...])
    for g in range(N_GROUP):
        spread[g] = chan_t[:, g * GROUP : (g + 1) * GROUP]

    def mask_group(g, _):
        rows = rows_at(g, G_ROWS)
        settle(w_buf.at[rows], load_sem.at[g])
        settle(miss_buf.at[rows], load_sem.at[N_GROUP + g])

        def mask_part(q, _):
            part = rows_at(g * GROUP + q, I_BLK)
            w_buf[part, :] = jnp.where(miss_buf[part, :] == 1, jnp.nan, w_buf[part, :])
            return 0

        lax.fori_loop(0, GROUP, mask_part, 0)
        return 0

    lax.fori_loop(0, N_GROUP, mask_group, 0)
    save = pltpu.make_async_copy(w_buf, w_ref, save_sem.at[0])
    save.start()
    await_greetings()
    send_ep(lambda peer: b_buf.at[b_mine], b_buf.at[b_mine], send_sem.at[0], recv_sem.at[0])
    send_tm(lambda peer: a_buf.at[a_mine], a_buf.at[a_mine], send_sem.at[1], recv_sem.at[1])
    me_mine = rows_at(t, A_OWN)
    mt_mine = rows_at(e, B_OWN)
    others_me_full = me_full.at[pl.ds(0, (N_TM - 1) * A_OWN)]
    others_mt_full = mt_full.at[pl.ds(0, (N_EP - 1) * B_OWN)]

    def start_gram_b():
        b = b_buf[...]
        bt_buf[...] = b.T
        store_slab(gb_part, bt_buf, e, 2 * PIECE, b)
        for h in range(2):
            send_tm(
                lambda peer: gb_part.at[h, rows_at(peer % N_X, PIECE)],
                gb_recv.at[h, rows_at(t, PIECE)],
                send_sem.at[2 + h],
                recv_sem.at[2 + h],
            )
            gb_recv[h, rows_at(t, PIECE), :] = gb_part[h, rows_at(x, PIECE), :]

    settle(others_b, recv_sem.at[0])
    start_gram_b()
    settle(others_a, recv_sem.at[1])
    acat[...] = pack_left(a_buf[...])
    settle(others_b, send_sem.at[0])
    settle(others_a, send_sem.at[1])

    def sweep(s, _):
        me_part[...] = jnp.zeros_like(me_part)

        def episode_group(g, _):
            for p in range(0, GROUP, 2):
                k = g * GROUP + p
                b_high, b_low = basis_pair(b_buf[...], chan_ref, k)
                model = model_pair(acat[...], b_high, b_low)
                highs, lows = [], []
                for d in range(2):
                    rows = rows_at(k + d, I_BLK)
                    w = w_buf[rows, :]
                    filled = jnp.where(w != w, model[:, d * J_BLK : (d + 1) * J_BLK], w)
                    high, low = split2(filled)
                    xh_buf[rows, :] = high
                    xl_buf[rows, :] = low
                    highs.append(high)
                    lows.append(low)
                high = jnp.concatenate(highs, axis=1)
                low = jnp.concatenate(lows, axis=1)
                me_part[...] += dot(
                    jnp.concatenate([high, low, high], axis=1),
                    jnp.concatenate([b_high, b_high, b_low], axis=0),
                )
            return 0

        lax.fori_loop(0, N_GROUP, episode_group, 0)
        me_slot = me_recv.at[rows_at(t, A_OWN)]
        send_tm(lambda peer: me_part.at[rows_at(peer, A_OWN)], me_slot, send_sem.at[6], recv_sem.at[6])
        me_recv[rows_at(t, A_OWN), :] = me_part[rows_at(t, A_OWN), :]
        gb_mine = rows_at(e * N_X + x, PIECE)
        for h in range(2):
            settle(others_gb[h], recv_sem.at[2 + h])
            gb_full[h, gb_mine, :] = sum_slots(gb_recv.at[h], N_TM, PIECE)
            mine = gb_full.at[h, gb_mine]
            send_layer(mine, mine, send_sem.at[4 + h], recv_sem.at[4 + h])
        settle(others_gb_full[0], recv_sem.at[4])
        form_half(s_buf, gb_full, gram_c, 0)

        def share_me():
            settle(others_me, recv_sem.at[6])
            me_full[me_mine, :] = sum_slots(me_recv, N_TM, A_OWN)
            mine = me_full.at[me_mine]
            send_tm(lambda peer: mine, mine, send_sem.at[7], recv_sem.at[7])

        eliminate_half(s_buf, 0, PANEL, share_me)
        settle(others_gb_full[1], recv_sem.at[5])
        form_half(s_buf, gb_full, gram_c, 1)
        finish_inverse(s_buf)
        settle(others_me_full, recv_sem.at[7])
        a = dot_high(me_full[...], s_buf[...])
        a_buf[...] = a

        at = a.T
        at_buf[...] = at
        store_slab(ga_part, at_buf, x, 4 * PIECE, a)
        for h in range(2):
            send_ep(
                lambda peer: ga_part.at[h, rows_at(peer, PIECE)],
                ga_recv.at[h, rows_at(e, PIECE)],
                send_sem.at[8 + h],
                recv_sem.at[8 + h],
            )
            ga_recv[h, rows_at(e, PIECE), :] = ga_part[h, rows_at(e, PIECE), :]
        acat[...] = pack_left(at_buf[...])
        for h in range(2):
            settle(others_gb[h], send_sem.at[2 + h])
            settle(others_gb_full[h], send_sem.at[4 + h])
        settle(others_me, send_sem.at[6])
        settle(others_me_full, send_sem.at[7])
        mt_acc[...] = jnp.zeros_like(mt_acc)

        def time_group(g, _):
            for p in range(0, GROUP, 2):
                k = g * GROUP + p
                high = jnp.concatenate([xh_buf[rows_at(k + d, I_BLK), :] for d in range(2)], axis=1)
                low = jnp.concatenate([xl_buf[rows_at(k + d, I_BLK), :] for d in range(2)], axis=1)
                prod = dot(acat[...], jnp.concatenate([high, high, low], axis=0))
                terms = [
                    jnp.broadcast_to(spread[g, :, p + d : p + d + 1], (RANK, J_BLK))
                    * prod[:, d * J_BLK : (d + 1) * J_BLK]
                    for d in range(2)
                ]
                mt_acc[...] += terms[0] + terms[1]
            return 0

        lax.fori_loop(0, N_GROUP, time_group, 0)
        mt_part[...] = mt_acc[...].T
        mt_slot = mt_recv.at[rows_at(e, B_OWN)]
        send_ep(lambda peer: mt_part.at[rows_at(peer, B_OWN)], mt_slot, send_sem.at[12], recv_sem.at[12])
        mt_recv[rows_at(e, B_OWN), :] = mt_part[rows_at(e, B_OWN), :]
        ga_mine = rows_at(x * N_EP + e, PIECE)
        for h in range(2):
            settle(others_ga[h], recv_sem.at[8 + h])
            ga_full[h, ga_mine, :] = sum_slots(ga_recv.at[h], N_EP, PIECE)
            mine = ga_full.at[h, ga_mine]
            send_layer(mine, mine, send_sem.at[10 + h], recv_sem.at[10 + h])
        settle(others_mt, recv_sem.at[12])
        mt_full[mt_mine, :] = sum_slots(mt_recv, N_EP, B_OWN)
        send_ep(lambda peer: mt_full.at[mt_mine], mt_full.at[mt_mine], send_sem.at[13], recv_sem.at[13])
        settle(others_ga_full[0], recv_sem.at[10])
        form_half(s_buf, ga_full, gram_c, 0)
        eliminate_half(s_buf, 0, PANEL)
        settle(others_ga_full[1], recv_sem.at[11])
        form_half(s_buf, ga_full, gram_c, 1)
        finish_inverse(s_buf)
        settle(others_mt_full, recv_sem.at[13])
        b_buf[...] = dot_high(mt_full[...], s_buf[...])
        for h in range(2):
            settle(others_ga[h], send_sem.at[8 + h])
            settle(others_ga_full[h], send_sem.at[10 + h])
        settle(others_mt, send_sem.at[12])
        settle(others_mt_full, send_sem.at[13])

        @pl.when(s < SWEEPS - 1)
        def _():
            start_gram_b()
            acat[...] = pack_left(a_buf[...])

        return 0

    lax.fori_loop(0, SWEEPS, sweep, 0)
    aout_ref[...] = a_buf[...]
    bout_ref[...] = b_buf[...]
    save.wait()


def store_slab(ref, turned, index, count, factor):
    rows = jnp.concatenate(
        [
            turned[pl.ds(pl.multiple_of(h * HALF + index * count, PIECE), count), :]
            for h in range(2)
        ],
        axis=0,
    )
    gram = dot_high(rows, factor)
    for h in range(2):
        for p in range(2 * count // PIECE):
            r, c = h * count + PIECE * (p // 2), HALF * (p % 2)
            ref[h, PIECE * p : PIECE * (p + 1), :] = gram[r : r + PIECE, c : c + HALF]


def form_half(s_ref, gram_ref, gram_c, h):
    row = lax.broadcasted_iota(jnp.int32, (PIECE, HALF), 0)
    lane = lax.broadcasted_iota(jnp.int32, (PIECE, HALF), 1)
    for p in range(N_PIECE):
        r, c = h * HALF + PIECE * (p // 2), HALF * (p % 2)
        part = gram_ref[h, PIECE * p : PIECE * (p + 1), :] * gram_c[r : r + PIECE, c : c + HALF]
        s_ref[r : r + PIECE, c : c + HALF] = part + jnp.where(row + r == lane + c, RIDGE, 0.0)


def finish_inverse(s_ref):
    eliminate_rows(s_ref, HALF, RANK, 0, HALF)
    eliminate_half(s_ref, HALF, PANEL)
    eliminate_rows(s_ref, 0, HALF, HALF, HALF)


def fit(obs, miss, a_own, b_own, channel):
    vmem = pl.BlockSpec(memory_space=pltpu.VMEM)
    anywhere = pl.BlockSpec(memory_space=pl.ANY)

    def f32(*shape):
        return pltpu.VMEM(shape, F32)

    return pl.pallas_call(
        fit_kernel,
        out_shape=(
            jax.ShapeDtypeStruct((ROWS, J_BLK), F32),
            jax.ShapeDtypeStruct((I_BLK, RANK), F32),
            jax.ShapeDtypeStruct((J_BLK, RANK), F32),
        ),
        in_specs=[anywhere, anywhere, vmem, vmem, vmem],
        out_specs=(anywhere, vmem, vmem),
        scratch_shapes=[
            f32(ROWS, J_BLK),
            pltpu.VMEM((ROWS, J_BLK), jnp.int32),
            pltpu.VMEM((ROWS, J_BLK), BF16),
            pltpu.VMEM((ROWS, J_BLK), BF16),
            f32(I_BLK, RANK),
            f32(J_BLK, RANK),
            pltpu.VMEM((I_BLK, 3 * RANK), BF16),
            f32(N_GROUP, RANK, GROUP),
            f32(RANK, RANK),
            f32(RANK, RANK),
            f32(RANK, J_BLK),
            f32(2, N_X * PIECE, HALF),
            f32(2, N_TM * PIECE, HALF),
            f32(2, N_PIECE * PIECE, HALF),
            f32(I_BLK, RANK),
            f32(I_BLK, RANK),
            f32(I_BLK, RANK),
            f32(RANK, I_BLK),
            f32(2, N_EP * PIECE, HALF),
            f32(2, N_EP * PIECE, HALF),
            f32(2, N_PIECE * PIECE, HALF),
            f32(J_BLK, RANK),
            f32(RANK, J_BLK),
            f32(J_BLK, RANK),
            f32(J_BLK, RANK),
            pltpu.SemaphoreType.DMA((2 * N_GROUP,)),
            pltpu.SemaphoreType.DMA((1,)),
            pltpu.SemaphoreType.DMA((14,)),
            pltpu.SemaphoreType.DMA((14,)),
        ],
        compiler_params=pltpu.CompilerParams(
            collective_id=0, has_side_effects=True, vmem_limit_bytes=VMEM_LIMIT
        ),
        name="fit",
    )(obs, miss, a_own, b_own, channel)


def complete_kernel(w_ref, a_ref, b_ref, chan_ref, out_ref, w_buf, acat, load_sem, save_sem):
    for g in range(N_GROUP):
        rows = pl.ds(g * G_ROWS, G_ROWS)
        pltpu.make_async_copy(w_ref.at[rows], w_buf.at[rows], load_sem.at[g]).start()
    acat[...] = pack_left(a_ref[...])

    for g in range(N_GROUP):
        settle(w_buf.at[pl.ds(g * G_ROWS, G_ROWS)], load_sem.at[g])
        for p in range(0, GROUP, 2):
            k = g * GROUP + p
            b_high, b_low = basis_pair(b_ref[...], chan_ref, k)
            model = model_pair(acat[...], b_high, b_low)
            for d in range(2):
                rows = pl.ds((k + d) * I_BLK, I_BLK)
                w = w_buf[rows, :]
                w_buf[rows, :] = jnp.where(w != w, model[:, d * J_BLK : (d + 1) * J_BLK], w)
                pltpu.make_async_copy(w_buf.at[rows], out_ref.at[:, k + d, :], save_sem.at[g]).start()
    for g in range(N_GROUP):
        settle(w_buf.at[pl.ds(g * G_ROWS, G_ROWS)], save_sem.at[g])


def complete(w, a_block, b_block, channel):
    vmem = pl.BlockSpec(memory_space=pltpu.VMEM)
    anywhere = pl.BlockSpec(memory_space=pl.ANY)
    return pl.pallas_call(
        complete_kernel,
        out_shape=jax.ShapeDtypeStruct((I_BLK, WIDTH, J_BLK), F32),
        in_specs=[anywhere, vmem, vmem, vmem],
        out_specs=anywhere,
        scratch_shapes=[
            pltpu.VMEM((ROWS, J_BLK), F32),
            pltpu.VMEM((I_BLK, 3 * RANK), BF16),
            pltpu.SemaphoreType.DMA((N_GROUP,)),
            pltpu.SemaphoreType.DMA((N_GROUP,)),
        ],
        compiler_params=pltpu.CompilerParams(vmem_limit_bytes=VMEM_LIMIT),
        name="complete",
    )(w, a_block, b_block, channel)


def on_device(observed, missing, episode_init, time_init, channel):
    obs = observed.transpose(0, 2, 1)
    miss = missing.transpose(0, 2, 1)
    w, a, b = fit(obs, miss, episode_init, time_init, channel)
    return complete(w, a, b, channel).transpose(0, 2, 1)


def solution(mesh):
    in_specs = (
        P("ep", "tm", None),
        P("ep", "tm", None),
        P(("ep", "tm"), None),
        P(("tm", "ep"), None),
        P(),
    )
    return jax.shard_map(
        on_device, mesh=mesh, in_specs=in_specs, out_specs=P("ep", "tm", None), check_vma=False
    )
```

```python
import jax
import jax.numpy as jnp
from jax import lax
from jax.experimental import pallas as pl
from jax.experimental.pallas import tpu as pltpu
from jax.sharding import PartitionSpec as P

SWEEPS = 2
RIDGE = 1.0
HIGH = lax.Precision.HIGHEST
F32 = jnp.float32
BF16 = jnp.bfloat16
MESH = pl.DeviceIdType.MESH

RANK = 256
WIDTH = 32
N_EP = 8
N_TM = 32
N_X = 4
I_BLK = 256
J_BLK = 128
ROWS = I_BLK * WIDTH
GROUP = 8
N_GROUP = WIDTH // GROUP
G_ROWS = GROUP * I_BLK
A_OWN = 8
B_OWN = 16
PIECE = 8
HALF = 128
PANEL = 16
N_PIECE = N_EP * N_X
VMEM_LIMIT = 56 * 1024 * 1024


def dot(left, right):
    return lax.dot_general(
        left, right, (((1,), (0,)), ((), ())), preferred_element_type=F32
    )


def dot_high(left, right):
    return lax.dot_general(
        left, right, (((1,), (0,)), ((), ())), precision=HIGH, preferred_element_type=F32
    )


def split2(x):
    high = x.astype(BF16)
    return high, (x - high.astype(F32)).astype(BF16)


def split3(x):
    high = x.astype(BF16)
    rest = x - high.astype(F32)
    mid = rest.astype(BF16)
    return high, mid, (rest - mid.astype(F32)).astype(BF16)


def dot_packed(left, right):
    a0, a1, a2 = split3(left)
    b0, b1, b2 = split3(right)
    lhs = jnp.concatenate([a0, a0, a1, a0, a2, a1], axis=1)
    rhs = jnp.concatenate([b0, b1, b0, b2, b0, b1], axis=0)
    return dot(lhs, rhs)


def invert8(cols):
    row = lax.broadcasted_iota(jnp.int32, (8, 128), 0)
    for s in range(8):
        here = row == s
        at_s = [jnp.broadcast_to(cols[q][s : s + 1, :], (8, 128)) for q in range(8)]
        inv = 1.0 / at_s[s]
        pivot = cols[s]
        fresh = []
        for q in range(8):
            if q == s:
                fresh.append(jnp.where(here, inv, -pivot * inv))
            else:
                scaled = at_s[q] * inv
                fresh.append(jnp.where(here, scaled, cols[q] - pivot * scaled))
        cols = fresh
    return cols


def spread_row(x, m):
    return jnp.broadcast_to(x[m : m + 1, :], (8, 128))


def eliminate_panel(ref, r0, depth, n):
    tiles = n // 128
    groups = depth // 8
    lane = lax.broadcasted_iota(jnp.int32, (8, 128), 1)
    row = lax.broadcasted_iota(jnp.int32, (8, 128), 0)
    x = [
        [ref[r0 + 8 * v : r0 + 8 * v + 8, 128 * t : 128 * t + 128] for t in range(tiles)]
        for v in range(groups)
    ]
    for g in range(groups):
        t_piv, l0 = divmod(r0 + 8 * g, 128)

        def column(block, q):
            return jnp.broadcast_to(block[:, l0 + q : l0 + q + 1], (8, 128))

        inv = invert8([column(x[g][t_piv], q) for q in range(8)])
        inside = (lane >= l0) & (lane < l0 + 8)
        unit = jnp.where(lane - l0 == row, 1.0, 0.0)
        fresh = []
        for t in range(tiles):
            old = x[g][t]
            if t == t_piv:
                old = jnp.where(inside, unit, old)
            y = [inv[m] * spread_row(old, m) for m in range(8)]
            fresh.append(((y[0] + y[1]) + (y[2] + y[3])) + ((y[4] + y[5]) + (y[6] + y[7])))
        for v in range(groups):
            if v == g:
                continue
            cols = [column(x[v][t_piv], m) for m in range(8)]
            for t in range(tiles):
                old = x[v][t]
                if t == t_piv:
                    old = jnp.where(inside, 0.0, old)
                y = [cols[m] * spread_row(fresh[t], m) for m in range(8)]
                x[v][t] = old - (
                    ((y[0] + y[1]) + (y[2] + y[3])) + ((y[4] + y[5]) + (y[6] + y[7]))
                )
        x[g] = fresh
    for v in range(groups):
        for t in range(tiles):
            ref[r0 + 8 * v : r0 + 8 * v + 8, 128 * t : 128 * t + 128] = x[v][t]


def eliminate_rows(ref, lo, hi, r0, depth):
    n = ref.shape[1]
    lane = lax.broadcasted_iota(jnp.int32, (1, n), 1)
    inside = (lane >= r0) & (lane < r0 + depth)
    product = dot_packed(ref[lo:hi, r0 : r0 + depth], ref[r0 : r0 + depth, :])
    ref[lo:hi, :] = jnp.where(inside, 0.0, ref[lo:hi, :]) - product


def eliminate_half(ref, base, depth, between=None):
    top = base + HALF
    for r0 in range(base, top, depth):
        eliminate_panel(ref, r0, depth, ref.shape[1])
        for lo, hi in ((base, r0), (r0 + depth, top)):
            if hi > lo:
                eliminate_rows(ref, lo, hi, r0, depth)
        if between is not None and r0 == base + 3 * depth:
            between()


def coords():
    e = lax.axis_index("ep")
    t = lax.axis_index("tm")
    return e, t, t // N_X, t % N_X


def greet():
    e, t, z, x = coords()
    barrier = pltpu.get_barrier_semaphore()

    def along_tm(k, _):
        peer = lax.rem(t + k, N_TM)
        pl.semaphore_signal(barrier, inc=1, device_id=(e, peer), device_id_type=MESH)
        return 0

    def in_layer(k, _):
        pe = lax.rem(e + k // N_X, N_EP)
        px = lax.rem(x + k % N_X, N_X)
        pl.semaphore_signal(barrier, inc=1, device_id=(pe, z * N_X + px), device_id_type=MESH)
        return 0

    lax.fori_loop(1, N_TM, along_tm, 0)
    lax.fori_loop(N_X, N_EP * N_X, in_layer, 0)


def await_greetings():
    pl.semaphore_wait(pltpu.get_barrier_semaphore(), N_TM - 1 + (N_EP - 1) * N_X)


def send_tm(src_of, dst, send_sem, recv_sem):
    e, t, _, _ = coords()

    def body(k, _):
        peer = lax.rem(t + k, N_TM)
        pltpu.make_async_remote_copy(
            src_ref=src_of(peer),
            dst_ref=dst,
            send_sem=send_sem,
            recv_sem=recv_sem,
            device_id=(e, peer),
            device_id_type=MESH,
        ).start()
        return 0

    lax.fori_loop(1, N_TM, body, 0)


def send_ep(src_of, dst, send_sem, recv_sem):
    e, t, _, _ = coords()

    def body(k, _):
        peer = lax.rem(e + k, N_EP)
        pltpu.make_async_remote_copy(
            src_ref=src_of(peer),
            dst_ref=dst,
            send_sem=send_sem,
            recv_sem=recv_sem,
            device_id=(peer, t),
            device_id_type=MESH,
        ).start()
        return 0

    lax.fori_loop(1, N_EP, body, 0)


def send_layer(src, dst, send_sem, recv_sem):
    e, _, z, x = coords()

    def body(k, _):
        pe = lax.rem(e + k // N_X, N_EP)
        px = lax.rem(x + k % N_X, N_X)
        pltpu.make_async_remote_copy(
            src_ref=src,
            dst_ref=dst,
            send_sem=send_sem,
            recv_sem=recv_sem,
            device_id=(pe, z * N_X + px),
            device_id_type=MESH,
        ).start()
        return 0

    lax.fori_loop(1, N_EP * N_X, body, 0)


def settle(ref, sem):
    pltpu.make_async_copy(ref, ref, sem).wait()


def sum_slots(ref, slots, rows):
    parts = [ref[rows * s : rows * (s + 1), :] for s in range(slots)]
    while len(parts) > 1:
        parts = [parts[i] + parts[i + 1] for i in range(0, len(parts), 2)]
    return parts[0]


def rows_at(index, size):
    return pl.ds(pl.multiple_of(index * size, size), size)


def dot_t(left, right):
    return lax.dot_general(
        left, right, (((1,), (1,)), ((), ())), preferred_element_type=F32
    )


def basis_pair(b, chan_ref, k):
    return split2(jnp.concatenate([b * chan_ref[pl.ds(k + d, 1), :] for d in range(2)], axis=0))


def model_pair(acat, high, low):
    return dot_t(acat, jnp.concatenate([high, high, low], axis=1))


def pack_left(x):
    high, low = split2(x)
    return jnp.concatenate([high, low, high], axis=1)


def fit_kernel(
    obs_ref,
    miss_ref,
    a_ref,
    b_ref,
    chan_ref,
    w_ref,
    aout_ref,
    bout_ref,
    w_buf,
    miss_buf,
    xh_buf,
    xl_buf,
    a_buf,
    b_buf,
    acat,
    spread,
    gram_c,
    s_buf,
    bt_buf,
    gb_part,
    gb_recv,
    gb_full,
    me_part,
    me_recv,
    me_full,
    at_buf,
    ga_part,
    ga_recv,
    ga_full,
    mt_part,
    mt_acc,
    mt_recv,
    mt_full,
    load_sem,
    save_sem,
    send_sem,
    recv_sem,
):
    e, t, z, x = coords()
    greet()
    for g in range(N_GROUP):
        for q in range(GROUP):
            k = g * GROUP + q
            to = pl.ds(k * I_BLK, I_BLK)
            pltpu.make_async_copy(obs_ref.at[:, k, :], w_buf.at[to], load_sem.at[g]).start()
            pltpu.make_async_copy(miss_ref.at[:, k, :], miss_buf.at[to], load_sem.at[N_GROUP + g]).start()
    a_mine = rows_at(t, A_OWN)
    b_mine = rows_at(e, B_OWN)
    a_buf[a_mine, :] = a_ref[...]
    b_buf[b_mine, :] = b_ref[...]
    others_a = a_buf.at[pl.ds(0, (N_TM - 1) * A_OWN)]
    others_b = b_buf.at[pl.ds(0, (N_EP - 1) * B_OWN)]
    others_gb = gb_recv.at[pl.ds(0, (N_TM - 1) * 2 * PIECE)]
    others_gb_full = [gb_full.at[h, pl.ds(0, (N_PIECE - 1) * PIECE)] for h in range(2)]
    others_me = me_recv.at[pl.ds(0, (N_TM - 1) * A_OWN)]
    others_ga = [ga_recv.at[h, pl.ds(0, (N_EP - 1) * PIECE)] for h in range(2)]
    others_ga_full = [ga_full.at[h, pl.ds(0, (N_PIECE - 1) * PIECE)] for h in range(2)]
    others_mt = mt_recv.at[pl.ds(0, (N_EP - 1) * B_OWN)]

    chan_t = chan_ref[...].T
    gram_c[...] = dot_high(chan_t, chan_ref[...])
    for g in range(N_GROUP):
        spread[g] = chan_t[:, g * GROUP : (g + 1) * GROUP]

    def mask_group(g, _):
        rows = rows_at(g, G_ROWS)
        settle(w_buf.at[rows], load_sem.at[g])
        settle(miss_buf.at[rows], load_sem.at[N_GROUP + g])

        def mask_part(q, _):
            part = rows_at(g * GROUP + q, I_BLK)
            w_buf[part, :] = jnp.where(miss_buf[part, :] == 1, jnp.nan, w_buf[part, :])
            return 0

        lax.fori_loop(0, GROUP, mask_part, 0)
        return 0

    lax.fori_loop(0, N_GROUP, mask_group, 0)
    save = pltpu.make_async_copy(w_buf, w_ref, save_sem.at[0])
    save.start()
    await_greetings()
    send_ep(lambda peer: b_buf.at[b_mine], b_buf.at[b_mine], send_sem.at[0], recv_sem.at[0])
    send_tm(lambda peer: a_buf.at[a_mine], a_buf.at[a_mine], send_sem.at[1], recv_sem.at[1])
    me_mine = rows_at(t, A_OWN)
    mt_mine = rows_at(e, B_OWN)
    others_me_full = me_full.at[pl.ds(0, (N_TM - 1) * A_OWN)]
    others_mt_full = mt_full.at[pl.ds(0, (N_EP - 1) * B_OWN)]

    def start_gram_b():
        b = b_buf[...]
        bt_buf[...] = b.T
        gram = slab_gram(bt_buf, e, 2 * PIECE, b)
        for p in range(N_X):
            for h in range(2):
                r, c = h * 2 * PIECE + PIECE * (p // 2), HALF * (p % 2)
                to = PIECE * (2 * p + h)
                gb_part[to : to + PIECE, :] = gram[r : r + PIECE, c : c + HALF]
        slot = rows_at(t, 2 * PIECE)
        send_tm(
            lambda peer: gb_part.at[rows_at(peer % N_X, 2 * PIECE)],
            gb_recv.at[slot],
            send_sem.at[2],
            recv_sem.at[2],
        )
        gb_recv[slot, :] = gb_part[rows_at(x, 2 * PIECE), :]

    settle(others_b, recv_sem.at[0])
    start_gram_b()
    settle(others_a, recv_sem.at[1])
    acat[...] = pack_left(a_buf[...])
    settle(others_b, send_sem.at[0])
    settle(others_a, send_sem.at[1])

    def sweep(s, _):
        me_part[...] = jnp.zeros_like(me_part)

        def episode_group(g, _):
            for p in range(0, GROUP, 2):
                k = g * GROUP + p
                b_high, b_low = basis_pair(b_buf[...], chan_ref, k)
                model = model_pair(acat[...], b_high, b_low)
                highs, lows = [], []
                for d in range(2):
                    rows = rows_at(k + d, I_BLK)
                    w = w_buf[rows, :]
                    filled = jnp.where(w != w, model[:, d * J_BLK : (d + 1) * J_BLK], w)
                    high, low = split2(filled)
                    xh_buf[rows, :] = high
                    xl_buf[rows, :] = low
                    highs.append(high)
                    lows.append(low)
                high = jnp.concatenate(highs, axis=1)
                low = jnp.concatenate(lows, axis=1)
                me_part[...] += dot(
                    jnp.concatenate([high, low, high], axis=1),
                    jnp.concatenate([b_high, b_high, b_low], axis=0),
                )
            return 0

        lax.fori_loop(0, N_GROUP, episode_group, 0)
        me_slot = me_recv.at[rows_at(t, A_OWN)]
        send_tm(lambda peer: me_part.at[rows_at(peer, A_OWN)], me_slot, send_sem.at[6], recv_sem.at[6])
        me_recv[rows_at(t, A_OWN), :] = me_part[rows_at(t, A_OWN), :]
        gb_mine = rows_at(e * N_X + x, PIECE)
        settle(others_gb, recv_sem.at[2])
        both = sum_slots(gb_recv, N_TM, 2 * PIECE)
        for h in range(2):
            gb_full[h, gb_mine, :] = both[h * PIECE : (h + 1) * PIECE, :]
            mine = gb_full.at[h, gb_mine]
            send_layer(mine, mine, send_sem.at[4 + h], recv_sem.at[4 + h])
        settle(others_gb_full[0], recv_sem.at[4])
        form_half(s_buf, gb_full, gram_c, 0)

        def share_me():
            settle(others_me, recv_sem.at[6])
            me_full[me_mine, :] = sum_slots(me_recv, N_TM, A_OWN)
            mine = me_full.at[me_mine]
            send_tm(lambda peer: mine, mine, send_sem.at[7], recv_sem.at[7])

        eliminate_half(s_buf, 0, PANEL, share_me)
        settle(others_gb_full[1], recv_sem.at[5])
        form_half(s_buf, gb_full, gram_c, 1)
        finish_inverse(s_buf)
        settle(others_me_full, recv_sem.at[7])
        a = dot_high(me_full[...], s_buf[...])
        a_buf[...] = a

        at = a.T
        at_buf[...] = at
        store_slab(ga_part, at_buf, x, 4 * PIECE, a)
        for h in range(2):
            send_ep(
                lambda peer: ga_part.at[h, rows_at(peer, PIECE)],
                ga_recv.at[h, rows_at(e, PIECE)],
                send_sem.at[8 + h],
                recv_sem.at[8 + h],
            )
            ga_recv[h, rows_at(e, PIECE), :] = ga_part[h, rows_at(e, PIECE), :]
        acat[...] = pack_left(at_buf[...])
        settle(others_gb, send_sem.at[2])
        for h in range(2):
            settle(others_gb_full[h], send_sem.at[4 + h])
        settle(others_me, send_sem.at[6])
        settle(others_me_full, send_sem.at[7])
        mt_acc[...] = jnp.zeros_like(mt_acc)

        def time_group(g, _):
            for p in range(0, GROUP, 2):
                k = g * GROUP + p
                high = jnp.concatenate([xh_buf[rows_at(k + d, I_BLK), :] for d in range(2)], axis=1)
                low = jnp.concatenate([xl_buf[rows_at(k + d, I_BLK), :] for d in range(2)], axis=1)
                prod = dot(acat[...], jnp.concatenate([high, high, low], axis=0))
                terms = [
                    jnp.broadcast_to(spread[g, :, p + d : p + d + 1], (RANK, J_BLK))
                    * prod[:, d * J_BLK : (d + 1) * J_BLK]
                    for d in range(2)
                ]
                mt_acc[...] += terms[0] + terms[1]
            return 0

        lax.fori_loop(0, N_GROUP, time_group, 0)
        mt_part[...] = mt_acc[...].T
        mt_slot = mt_recv.at[rows_at(e, B_OWN)]
        send_ep(lambda peer: mt_part.at[rows_at(peer, B_OWN)], mt_slot, send_sem.at[12], recv_sem.at[12])
        mt_recv[rows_at(e, B_OWN), :] = mt_part[rows_at(e, B_OWN), :]
        ga_mine = rows_at(x * N_EP + e, PIECE)
        for h in range(2):
            settle(others_ga[h], recv_sem.at[8 + h])
            ga_full[h, ga_mine, :] = sum_slots(ga_recv.at[h], N_EP, PIECE)
            mine = ga_full.at[h, ga_mine]
            send_layer(mine, mine, send_sem.at[10 + h], recv_sem.at[10 + h])
        settle(others_mt, recv_sem.at[12])
        mt_full[mt_mine, :] = sum_slots(mt_recv, N_EP, B_OWN)
        send_ep(lambda peer: mt_full.at[mt_mine], mt_full.at[mt_mine], send_sem.at[13], recv_sem.at[13])
        settle(others_ga_full[0], recv_sem.at[10])
        form_half(s_buf, ga_full, gram_c, 0)
        eliminate_half(s_buf, 0, PANEL)
        settle(others_ga_full[1], recv_sem.at[11])
        form_half(s_buf, ga_full, gram_c, 1)
        finish_inverse(s_buf)
        settle(others_mt_full, recv_sem.at[13])
        b_buf[...] = dot_high(mt_full[...], s_buf[...])
        for h in range(2):
            settle(others_ga[h], send_sem.at[8 + h])
            settle(others_ga_full[h], send_sem.at[10 + h])
        settle(others_mt, send_sem.at[12])
        settle(others_mt_full, send_sem.at[13])

        @pl.when(s < SWEEPS - 1)
        def _():
            start_gram_b()
            acat[...] = pack_left(a_buf[...])

        return 0

    lax.fori_loop(0, SWEEPS, sweep, 0)
    aout_ref[...] = a_buf[...]
    bout_ref[...] = b_buf[...]
    save.wait()


def store_slab(ref, turned, index, count, factor):
    gram = slab_gram(turned, index, count, factor)
    for h in range(2):
        for p in range(2 * count // PIECE):
            r, c = h * count + PIECE * (p // 2), HALF * (p % 2)
            ref[h, PIECE * p : PIECE * (p + 1), :] = gram[r : r + PIECE, c : c + HALF]


def slab_gram(turned, index, count, factor):
    rows = jnp.concatenate(
        [
            turned[pl.ds(pl.multiple_of(h * HALF + index * count, PIECE), count), :]
            for h in range(2)
        ],
        axis=0,
    )
    return dot_high(rows, factor)


def form_half(s_ref, gram_ref, gram_c, h):
    row = lax.broadcasted_iota(jnp.int32, (PIECE, HALF), 0)
    lane = lax.broadcasted_iota(jnp.int32, (PIECE, HALF), 1)
    for p in range(N_PIECE):
        r, c = h * HALF + PIECE * (p // 2), HALF * (p % 2)
        part = gram_ref[h, PIECE * p : PIECE * (p + 1), :] * gram_c[r : r + PIECE, c : c + HALF]
        s_ref[r : r + PIECE, c : c + HALF] = part + jnp.where(row + r == lane + c, RIDGE, 0.0)


def finish_inverse(s_ref):
    eliminate_rows(s_ref, HALF, RANK, 0, HALF)
    eliminate_half(s_ref, HALF, PANEL)
    eliminate_rows(s_ref, 0, HALF, HALF, HALF)


def fit(obs, miss, a_own, b_own, channel):
    vmem = pl.BlockSpec(memory_space=pltpu.VMEM)
    anywhere = pl.BlockSpec(memory_space=pl.ANY)

    def f32(*shape):
        return pltpu.VMEM(shape, F32)

    return pl.pallas_call(
        fit_kernel,
        out_shape=(
            jax.ShapeDtypeStruct((ROWS, J_BLK), F32),
            jax.ShapeDtypeStruct((I_BLK, RANK), F32),
            jax.ShapeDtypeStruct((J_BLK, RANK), F32),
        ),
        in_specs=[anywhere, anywhere, vmem, vmem, vmem],
        out_specs=(anywhere, vmem, vmem),
        scratch_shapes=[
            f32(ROWS, J_BLK),
            pltpu.VMEM((ROWS, J_BLK), jnp.int32),
            pltpu.VMEM((ROWS, J_BLK), BF16),
            pltpu.VMEM((ROWS, J_BLK), BF16),
            f32(I_BLK, RANK),
            f32(J_BLK, RANK),
            pltpu.VMEM((I_BLK, 3 * RANK), BF16),
            f32(N_GROUP, RANK, GROUP),
            f32(RANK, RANK),
            f32(RANK, RANK),
            f32(RANK, J_BLK),
            f32(N_X * 2 * PIECE, HALF),
            f32(N_TM * 2 * PIECE, HALF),
            f32(2, N_PIECE * PIECE, HALF),
            f32(I_BLK, RANK),
            f32(I_BLK, RANK),
            f32(I_BLK, RANK),
            f32(RANK, I_BLK),
            f32(2, N_EP * PIECE, HALF),
            f32(2, N_EP * PIECE, HALF),
            f32(2, N_PIECE * PIECE, HALF),
            f32(J_BLK, RANK),
            f32(RANK, J_BLK),
            f32(J_BLK, RANK),
            f32(J_BLK, RANK),
            pltpu.SemaphoreType.DMA((2 * N_GROUP,)),
            pltpu.SemaphoreType.DMA((1,)),
            pltpu.SemaphoreType.DMA((14,)),
            pltpu.SemaphoreType.DMA((14,)),
        ],
        compiler_params=pltpu.CompilerParams(
            collective_id=0, has_side_effects=True, vmem_limit_bytes=VMEM_LIMIT
        ),
        name="fit",
    )(obs, miss, a_own, b_own, channel)


def complete_kernel(w_ref, a_ref, b_ref, chan_ref, out_ref, w_buf, acat, load_sem, save_sem):
    for g in range(N_GROUP):
        rows = pl.ds(g * G_ROWS, G_ROWS)
        pltpu.make_async_copy(w_ref.at[rows], w_buf.at[rows], load_sem.at[g]).start()
    acat[...] = pack_left(a_ref[...])

    for g in range(N_GROUP):
        settle(w_buf.at[pl.ds(g * G_ROWS, G_ROWS)], load_sem.at[g])
        for p in range(0, GROUP, 2):
            k = g * GROUP + p
            b_high, b_low = basis_pair(b_ref[...], chan_ref, k)
            model = model_pair(acat[...], b_high, b_low)
            for d in range(2):
                rows = pl.ds((k + d) * I_BLK, I_BLK)
                w = w_buf[rows, :]
                w_buf[rows, :] = jnp.where(w != w, model[:, d * J_BLK : (d + 1) * J_BLK], w)
                pltpu.make_async_copy(w_buf.at[rows], out_ref.at[:, k + d, :], save_sem.at[g]).start()
    for g in range(N_GROUP):
        settle(w_buf.at[pl.ds(g * G_ROWS, G_ROWS)], save_sem.at[g])


def complete(w, a_block, b_block, channel):
    vmem = pl.BlockSpec(memory_space=pltpu.VMEM)
    anywhere = pl.BlockSpec(memory_space=pl.ANY)
    return pl.pallas_call(
        complete_kernel,
        out_shape=jax.ShapeDtypeStruct((I_BLK, WIDTH, J_BLK), F32),
        in_specs=[anywhere, vmem, vmem, vmem],
        out_specs=anywhere,
        scratch_shapes=[
            pltpu.VMEM((ROWS, J_BLK), F32),
            pltpu.VMEM((I_BLK, 3 * RANK), BF16),
            pltpu.SemaphoreType.DMA((N_GROUP,)),
            pltpu.SemaphoreType.DMA((N_GROUP,)),
        ],
        compiler_params=pltpu.CompilerParams(vmem_limit_bytes=VMEM_LIMIT),
        name="complete",
    )(w, a_block, b_block, channel)


def on_device(observed, missing, episode_init, time_init, channel):
    obs = observed.transpose(0, 2, 1)
    miss = missing.transpose(0, 2, 1)
    w, a, b = fit(obs, miss, episode_init, time_init, channel)
    return complete(w, a, b, channel).transpose(0, 2, 1)


def solution(mesh):
    in_specs = (
        P("ep", "tm", None),
        P("ep", "tm", None),
        P(("ep", "tm"), None),
        P(("tm", "ep"), None),
        P(),
    )
    return jax.shard_map(
        on_device, mesh=mesh, in_specs=in_specs, out_specs=P("ep", "tm", None), check_vma=False
    )
```
